128 devices in a mesh: dp: 16 (over y, x), seq: 8 (over z, core).
Axes of the slice: x: 4, y: 4, z: 4, core: 2. Of those that a mesh axis runs over, the one named last changes fastest.
Arguments:
- activations: bfloat16 [16, 1024, 1536], P('dp', 'seq'), may hold values from -6 to 6
- convolution_weight: bfloat16 [5, 1536, 384], replicated, may hold values from -0.0625 to 0.0625
- out_weight: bfloat16 [384, 1536], replicated, may hold values from -0.3125 to 0.3125
- cotangent: bfloat16 [16, 1024, 1536], P('dp', 'seq'), may hold values from -6 to 6
- donor_pos: int32 [16, 448], P('dp'), may hold values from 0 to 1023, as said below
- acceptor_pos: int32 [16, 448], P('dp'), may hold values from 0 to 1023, as said below
- junction_flags: int32 [16, 448], P('dp'), may hold values 0 or 1
- junction_grad: float32 [16, 448], P('dp'), may hold values from -72 to 72
Outputs:
- block_out: bfloat16 [16, 1024, 1536], P('dp', 'seq')
- input_grad: bfloat16 [16, 1024, 1536], P('dp', 'seq')
- conv_grad: float32 [5, 1536, 384], P(None, ('dp', 'seq'))
- out_grad: float32 [384, 1536], P(('dp', 'seq'))
The draws below stay inside these ranges and needn't reach their ends.
Inputs may be any that keep to these rules, and one draw needn't show every extreme that they name: `donor_pos`: of each sequence's entries, exactly 56 have their donor among the 128 positions of each device. For two devices along seq, at most 16 entries have their donor on the first and their acceptor on the second, and for every first device exactly 16 for some second device. Padding entries carry positions too. `acceptor_pos`: the acceptor of an entry may lie before or after its donor, on any device.
All inputs are finite; a program needn't handle non-finite values. No bound on the sum of `junction_flags` on one device may be relied on, other than what follows from the above.
Results may differ from the reference program's by a relative error of at most 0.013.
Values may be sent and summed in bfloat16 or wider, within the bound.
A program may use at most 128 MiB of HBM per device.

```python
import jax
import jax.numpy as jnp
from jax import lax

C = 1536
CB = 384
KERNEL_WIDTH = 5
DILATION_STEP = 32
POS_DEV = 128
CAP = 16
JUNC_DEV = 56
SEQUENCE_LENGTH = 1024
B = 16
JUNC = 448


def junction_pairs(key):
    seq_count = JUNC // JUNC_DEV

    def one_device(base_key, device):
        key_order, key_shift, key_donor, key_accept = jax.random.split(base_key, 4)
        ordering = jnp.concatenate([jnp.arange(CAP), CAP + jax.random.permutation(key_order, 3 * CAP)[:JUNC_DEV - CAP]])
        classes = ordering // CAP
        offsets = jax.random.permutation(key_shift, seq_count)[:4]
        target = (device + offsets[classes]) % seq_count
        donors = device * POS_DEV + jax.random.randint(key_donor, (JUNC_DEV,), 0, POS_DEV)
        accepts = target * POS_DEV + jax.random.randint(key_accept, (JUNC_DEV,), 0, POS_DEV)
        return (donors.astype(jnp.int32), accepts.astype(jnp.int32))

    def one_sequence(seq_key):
        devices = jnp.arange(seq_count)
        donors, accepts = jax.vmap(lambda device: one_device(jax.random.fold_in(seq_key, device), device))(devices)
        shuffle = jax.random.permutation(jax.random.fold_in(seq_key, 1000003), JUNC)
        return (donors.reshape(-1)[shuffle], accepts.reshape(-1)[shuffle])
    return jax.vmap(one_sequence)(jax.random.split(key, B))


def draw_donor_pos(key, part):
    paired = junction_pairs(key)
    return paired[0]


def draw_acceptor_pos(key, part):
    paired = junction_pairs(key)
    return paired[1]


def with_ends(result, stream_key, smallest, high):
    shape = result.shape
    index_at = [jax.random.randint(jax.random.fold_in(stream_key, axis), (), 0, shape[axis]) for axis in range(len(shape))]
    result = result.at[tuple(index_at)].set(smallest)
    longest = shape.index(max(shape))
    index_at[longest] = (index_at[longest] + 1) % shape[longest]
    return result.at[tuple(index_at)].set(high)


def shard_levels(rng, extent, cuts, least, top_value):
    loudness, own = 1.0, jax.random.fold_in(rng, 6)
    for dim, blocks in cuts:
        draws = jnp.exp(jax.random.uniform(jax.random.fold_in(own, dim), (blocks,), jnp.float32, least / len(cuts), top_value / len(cuts)))
        loudness = loudness * jnp.repeat(draws, extent[dim] // blocks).reshape([-1 if axis == dim else 1 for axis in range(len(extent))])
    return loudness


def noise(key, shape, deviation, limit, cuts=(), kind=jnp.bfloat16):
    result = deviation * jax.random.normal(key, shape, jnp.float32)
    if cuts:
        result = result * shard_levels(key, shape, cuts, -0.22, 0.18)
    return jnp.clip(result, -limit, limit).astype(kind)


def setup_inputs(seed: int = 0) -> dict:
    splits = jax.random.split(jax.random.key(seed), 9)
    return {
        "activations": noise(splits[0], (B, SEQUENCE_LENGTH, C), 1.0, 6.0, ((0, 16), (1, 8))),
        "convolution_weight": noise(splits[1], (KERNEL_WIDTH, C, CB), (KERNEL_WIDTH * C) ** -0.5, 0.0625),
        "out_weight": noise(splits[2], (CB, C), CB ** -0.5, 0.3125),
        "cotangent": noise(splits[3], (B, SEQUENCE_LENGTH, C), 1.0, 6.0, ((0, 16), (1, 8))),
        "donor_pos": draw_donor_pos(jax.random.fold_in(splits[8], 71), 0),
        "acceptor_pos": draw_acceptor_pos(jax.random.fold_in(splits[8], 71), 0),
        "junction_flags": with_ends((jax.random.randint(splits[6], (B, JUNC), 0, 4) < 3).astype(jnp.int32), jax.random.fold_in(splits[6], 1), 0, 1),
        "junction_grad": noise(splits[7], (B, JUNC), 12.0, 72.0, ((0, 16),), jnp.float32),
    }


EPS = 1e-06
SLOPE = 0.7978845608028654
CUBIC = 0.044715

def gelu_tanh(values):
    return 0.5 * values * (1.0 + jnp.tanh(SLOPE * (values + CUBIC * values * values * values)))

def gelu_slope(values):
    curved = jnp.tanh(SLOPE * (values + CUBIC * values * values * values))
    return 0.5 * (1.0 + curved) + 0.5 * values * (1.0 - curved * curved) * SLOPE * (1.0 + 3.0 * CUBIC * values * values)

def reference(activations, convolution_weight, out_weight, cotangent, donor_pos, acceptor_pos, junction_flags, junction_grad):
    border_width = KERNEL_WIDTH // 2 * DILATION_STEP

    def one_sequence(running, pieces):
        seq_acts, seq_cotangent, donors, accepts, flag_row, grad_row = pieces
        act_float = seq_acts.astype(jnp.float32)
        inverse = lax.rsqrt(lax.optimization_barrier(jnp.mean(act_float * act_float, axis=-1, keepdims=True)) + EPS)
        normed = (act_float * inverse).astype(jnp.bfloat16)
        padded_input = jnp.pad(normed, ((border_width, border_width), (0, 0)))
        preactivation = jnp.zeros((SEQUENCE_LENGTH, CB), jnp.float32)
        for kernel_tap_index in range(KERNEL_WIDTH):
            preactivation = preactivation + jnp.dot(padded_input[kernel_tap_index * DILATION_STEP:kernel_tap_index * DILATION_STEP + SEQUENCE_LENGTH], convolution_weight[kernel_tap_index], preferred_element_type=jnp.float32)
        hidden = gelu_tanh(preactivation).astype(jnp.bfloat16)
        block_out = (act_float + jnp.dot(hidden, out_weight, preferred_element_type=jnp.float32)).astype(jnp.bfloat16)
        embedding = block_out.astype(jnp.float32)
        scaled = grad_row * flag_row.astype(jnp.float32) * C ** (-0.5)
        pulled = jnp.zeros((SEQUENCE_LENGTH, C), jnp.float32)
        pulled = pulled.at[donors].add(scaled[:, None] * embedding[accepts])
        pulled = pulled.at[accepts].add(scaled[:, None] * embedding[donors])
        upstream = (seq_cotangent.astype(jnp.float32) + pulled).astype(jnp.bfloat16)
        grad_hidden = jnp.dot(upstream, out_weight.T, preferred_element_type=jnp.float32)
        preactivation_gradient = (grad_hidden * gelu_slope(preactivation)).astype(jnp.bfloat16)
        out_term = jnp.dot(hidden.T, upstream, preferred_element_type=jnp.float32)
        grad_pad = jnp.pad(preactivation_gradient, ((border_width, border_width), (0, 0)))
        grad_normed = jnp.zeros((SEQUENCE_LENGTH, C), jnp.float32)
        convolution_terms = []
        for kernel_tap_index in range(KERNEL_WIDTH):
            offset_start = (KERNEL_WIDTH - 1 - kernel_tap_index) * DILATION_STEP
            grad_normed = grad_normed + jnp.dot(grad_pad[offset_start:offset_start + SEQUENCE_LENGTH], convolution_weight[kernel_tap_index].T, preferred_element_type=jnp.float32)
            convolution_terms.append(jnp.dot(padded_input[kernel_tap_index * DILATION_STEP:kernel_tap_index * DILATION_STEP + SEQUENCE_LENGTH].T, preactivation_gradient, preferred_element_type=jnp.float32))
        spread = lax.optimization_barrier(jnp.mean(grad_normed * act_float, axis=-1, keepdims=True))
        input_grad = (upstream.astype(jnp.float32) + inverse * grad_normed - inverse * inverse * inverse * act_float * spread).astype(jnp.bfloat16)
        conv_sum, out_sum = running
        return ((conv_sum + jnp.stack(convolution_terms), out_sum + out_term), (block_out, input_grad))
    initial = (jnp.zeros((KERNEL_WIDTH, C, CB), jnp.float32), jnp.zeros((CB, C), jnp.float32))
    totals, outputs = lax.scan(one_sequence, initial, (activations, cotangent, donor_pos, acceptor_pos, junction_flags, junction_grad))
    return (outputs[0], outputs[1], totals[0], totals[1])
```

```python
import itertools

import jax
import jax.numpy as jnp
from jax import lax
from jax.experimental import pallas as pl
from jax.experimental.pallas import tpu as pltpu
from jax.sharding import PartitionSpec as P

C = 1536
M = 384
TAPS = 5
STEP = 32
ROWS = 128
SEQ = 8
LENGTH = ROWS * SEQ
EDGE = TAPS // 2 * STEP
CAP = 16
JUNC = 448
PAIR = 2 * CAP
SLOTS = SEQ * PAIR
SIDE = 4
DP = SIDE * SIDE
OWNED = 12
BAND = 16

EPS = 1e-06
SLOPE = 0.7978845608028654
CUBIC = 0.044715

MESH = pl.DeviceIdType.MESH
bf16 = jnp.bfloat16
f32 = jnp.float32
i32 = jnp.int32


def dot(a, b):
    return jnp.dot(a, b, preferred_element_type=f32)


def dot_nt(a, b):
    return lax.dot_general(a, b, (((1,), (1,)), ((), ())), preferred_element_type=f32)


def dot_tn(a, b):
    return lax.dot_general(a, b, (((0,), (0,)), ((), ())), preferred_element_type=f32)


def one_hot(count, row):
    return lax.broadcasted_iota(i32, (count, row.shape[1]), 0) == row


def ones_of(mask):
    return jnp.where(mask, 1.0, 0.0).astype(bf16)


def gelu_parts(v):
    curved = jnp.tanh(SLOPE * (v + CUBIC * v * v * v))
    hidden = 0.5 * v * (1.0 + curved)
    slope = 0.5 * (1.0 + curved) + 0.5 * v * (1.0 - curved * curved) * SLOPE * (
        1.0 + 3.0 * CUBIC * v * v
    )
    return hidden, slope


def junction_matrices(s, don, acc, flags, grad):
    scaled = grad * flags.astype(f32) * C ** (-0.5)
    high = scaled.astype(bf16)
    low = (scaled - high.astype(f32)).astype(bf16)
    don_owner = don >> 7
    acc_owner = acc >> 7
    pairs = ones_of(one_hot(SEQ * SEQ, don_owner * SEQ + acc_owner))
    earlier = ones_of(
        lax.broadcasted_iota(i32, (JUNC, JUNC), 0) < lax.broadcasted_iota(i32, (JUNC, JUNC), 1)
    )
    counts = dot(pairs, earlier)
    rank = jnp.sum(pairs.astype(f32) * counts, axis=0, keepdims=True).astype(i32)
    don_here = don_owner == s
    acc_here = acc_owner == s
    don_at = one_hot(ROWS, don - s * ROWS)
    acc_at = one_hot(ROWS, acc - s * ROWS)
    send_don = ones_of(one_hot(SLOTS, jnp.where(don_here, acc_owner * PAIR + rank, -1)))
    send_acc = ones_of(one_hot(SLOTS, jnp.where(acc_here, don_owner * PAIR + CAP + rank, -1)))
    select = (dot_nt(send_don, ones_of(don_at)) + dot_nt(send_acc, ones_of(acc_at))).astype(bf16)
    came_don = ones_of(one_hot(SLOTS, jnp.where(acc_here, don_owner * PAIR + rank, -1)))
    came_acc = ones_of(one_hot(SLOTS, jnp.where(don_here, acc_owner * PAIR + CAP + rank, -1)))

    def placing(weight):
        wide = weight.astype(f32)
        at_acc = jnp.where(acc_at, wide, 0.0).astype(bf16)
        at_don = jnp.where(don_at, wide, 0.0).astype(bf16)
        return (dot_nt(at_acc, came_don) + dot_nt(at_don, came_acc)).astype(bf16)

    return select, placing(high), placing(low)


def kernel(
    act_hbm,
    w_hbm,
    ow_hbm,
    cot_hbm,
    don_hbm,
    acc_hbm,
    flag_hbm,
    grad_hbm,
    block_hbm,
    input_hbm,
    conv_hbm,
    out_hbm,
    act,
    w,
    ow,
    cot,
    don,
    acc,
    flag,
    grad,
    npad,
    xsend,
    xall,
    gsend,
    grecv,
    hsend,
    hrecv,
    bsend,
    brecv,
    gall,
    cbuf,
    c1,
    c2,
    c3,
    osend,
    osib,
    obuf,
    o1,
    o2,
    o3,
    oz,
    ozr,
    block,
    result,
    cout,
    oout,
    lsem,
    ssem,
    rsem,
):
    s = lax.axis_index("seq")
    d = lax.axis_index("dp")
    z, core = s // 2, s % 2
    y, x = d // SIDE, d % SIDE
    sibling = s + 1 - 2 * core
    ids = itertools.count()
    pending = []

    def push(src, dst, **device):
        i = next(ids)
        copy = pltpu.make_async_remote_copy(
            src_ref=src,
            dst_ref=dst,
            send_sem=ssem.at[i],
            recv_sem=rsem.at[i],
            device_id=device,
            device_id_type=MESH,
        )
        copy.start()
        pending.append(copy)
        return copy

    def seq_at(step):
        return lax.rem(s + step, SEQ)

    def x_at(step):
        return lax.rem(x + step, SIDE)

    def y_at(step):
        return lax.rem(y + step, SIDE)

    loads = {}
    for i, (name, src, dst) in enumerate(
        (
            ("act", act_hbm.at[0], act),
            ("don", don_hbm, don),
            ("acc", acc_hbm, acc),
            ("flag", flag_hbm, flag),
            ("grad", grad_hbm, grad),
            ("ow", ow_hbm, ow),
            ("w", w_hbm, w),
            ("cot", cot_hbm.at[0], cot),
        )
    ):
        loads[name] = pltpu.make_async_copy(src, dst, lsem.at[i])
        loads[name].start()

    barrier = pltpu.get_barrier_semaphore()
    for step in range(1, SEQ):
        pl.semaphore_signal(barrier, inc=1, device_id={"seq": seq_at(step)}, device_id_type=MESH)
    for step in range(1, SIDE):
        pl.semaphore_signal(
            barrier, inc=1, device_id={"dp": y * SIDE + x_at(step)}, device_id_type=MESH
        )
        pl.semaphore_signal(
            barrier, inc=1, device_id={"dp": y_at(step) * SIDE + x}, device_id_type=MESH
        )

    gall[0:EDGE] = jnp.zeros((EDGE, M), bf16)
    gall[EDGE + LENGTH :] = jnp.zeros((EDGE, M), bf16)

    loads["act"].wait()
    act_float = act[...].astype(f32)
    inverse = lax.rsqrt(jnp.mean(act_float * act_float, axis=-1, keepdims=True) + EPS)
    npad[EDGE : EDGE + ROWS] = (act_float * inverse).astype(bf16)
    pl.semaphore_wait(barrier, SEQ - 1 + 2 * (SIDE - 1))
    ahead = push(npad.at[ROWS : ROWS + EDGE], npad.at[0:EDGE], seq=seq_at(1))
    behind = push(npad.at[EDGE : 2 * EDGE], npad.at[EDGE + ROWS :], seq=seq_at(SEQ - 1))

    for name in ("don", "acc", "flag", "grad"):
        loads[name].wait()
    select, place_high, place_low = junction_matrices(s, don[...], acc[...], flag[...], grad[...])

    def own_block(ref):
        return ref.at[pl.ds(pl.multiple_of(s * PAIR, PAIR), PAIR)]

    def send_slots(rows, out, into):
        out[...] = dot(select, rows).astype(bf16)
        own_block(into)[...] = own_block(out)[...]
        copies = []
        for step in (1, 7, 2, 6, 3, 5, 4):
            peer = seq_at(step)
            src = out.at[pl.ds(pl.multiple_of(peer * PAIR, PAIR), PAIR)]
            copies.append(push(src, own_block(into), seq=peer))
        return copies

    def placed(ref):
        return dot(place_high, ref[...]) + dot(place_low, ref[...])

    loads["ow"].wait()
    ow_value = ow[...]
    act_back = dot_nt(act[...], ow_value).astype(bf16)
    act_slots = send_slots(act_back, gsend, grecv)

    loads["w"].wait()
    preact = dot(npad[EDGE : EDGE + ROWS], w[TAPS // 2])
    ahead.wait_recv()
    behind.wait_recv()

    @pl.when(s == 0)
    def _():
        npad[0:EDGE] = jnp.zeros((EDGE, C), bf16)

    @pl.when(s == SEQ - 1)
    def _():
        npad[EDGE + ROWS :] = jnp.zeros((EDGE, C), bf16)

    for tap in (0, 1, 3, 4):
        preact = preact + dot(npad[tap * STEP : tap * STEP + ROWS], w[tap])
    hidden_float, slope = gelu_parts(preact)
    hidden = hidden_float.astype(bf16)
    hidden_slots = send_slots(hidden, hsend, hrecv)

    column = lax.broadcasted_iota(i32, (1, SEQ * ROWS), 1)
    band_row = column % BAND
    wanted = jnp.where(
        band_row < OWNED,
        (column % ROWS) // BAND * (OWNED * SEQ) + column // ROWS * OWNED + band_row,
        -1,
    )
    regroup = ones_of(one_hot(C // 2, wanted))
    for half in range(2):
        part = dot(npad[EDGE : EDGE + ROWS, half * (C // 2) : (half + 1) * (C // 2)], regroup)
        for peer in range(SEQ):
            xsend[peer, :, half * ROWS : (half + 1) * ROWS] = part[
                :, peer * ROWS : (peer + 1) * ROWS
            ].astype(bf16)
    here = pl.ds(pl.multiple_of(s * ROWS, ROWS), ROWS)
    xall[here] = xsend[s]
    x_copies = [
        push(xsend.at[seq_at(step)], xall.at[here], seq=seq_at(step))
        for step in (1, 7, 2, 6, 3, 5, 4)
    ]

    block[...] = (act[...].astype(f32) + dot(hidden, ow_value)).astype(bf16)
    block_store = pltpu.make_async_copy(block, block_hbm.at[0], lsem.at[8])
    block_store.start()
    loads["cot"].wait()
    cot_back = dot_nt(cot[...], ow_value)
    ow_square = dot_nt(ow_value, ow_value).astype(bf16)

    for copy in act_slots:
        copy.wait_recv()
    cot_back = cot_back + placed(grecv)
    for copy in hidden_slots:
        copy.wait_recv()
    mixed = placed(hrecv).astype(bf16)
    grad_hidden = cot_back + dot(mixed, ow_square)
    grad_here = pl.ds(pl.multiple_of(EDGE + s * ROWS, EDGE), ROWS)
    gall[grad_here] = (grad_hidden * slope).astype(bf16)

    def chunk(owner):
        return gall.at[pl.ds(pl.multiple_of(EDGE + owner * ROWS, EDGE), ROWS)]

    along = [push(chunk(s), chunk(s), seq=seq_at(2 * step)) for step in (1, 3, 2)]
    across = [push(chunk(s), chunk(s), seq=sibling)]

    slot = lax.broadcasted_iota(i32, (1, 2 * DP * BAND), 1)
    within = slot % BAND
    third = (within * 11) >> 5
    wanted = jnp.where(
        within < OWNED,
        (slot % (DP * BAND)) // BAND * (3 * SEQ)
        + third * 6
        + slot // (DP * BAND) * 3
        + within
        - third * 3,
        -1,
    )
    order = ones_of(one_hot(M, wanted))
    hidden_order = dot(hidden, order).astype(bf16)
    mixed_order = dot(mixed, order).astype(bf16)
    terms = dot_tn(hidden_order, cot[...]) + dot_tn(mixed_order, block[...])
    osend[...] = terms.astype(bf16).reshape(2, SIDE, SIDE, BAND, C)
    to_sibling = push(osend.at[1 - core], osib, seq=sibling)

    for step, copy in zip((1, 3, 2), along):
        copy.wait_recv()
        owner = lax.rem(s + SEQ - 2 * step, SEQ)
        across.append(push(chunk(owner), chunk(owner), seq=sibling))

    block_slots = send_slots(block[...], bsend, brecv)

    to_sibling.wait_recv()
    obuf[...] = (osend[core].astype(f32) + osib[...].astype(f32)).astype(bf16)
    out_first = [
        push(obuf.at[y_at(step)], o1.at[step - 1], dp=y_at(step) * SIDE + x)
        for step in range(1, SIDE)
    ]

    for copy in x_copies:
        copy.wait_recv()
    for copy in across:
        copy.wait_recv()

    conv_first = []
    for tap in range(TAPS):
        start = 2 * EDGE - tap * STEP
        term = dot_tn(xall[...], gall[start : start + LENGTH])
        cbuf[tap] = term.astype(bf16).reshape(SIDE, SIDE, BAND, M)
        copies = []
        for step in range(1, SIDE):
            if tap % 2 == 0:
                copies.append(
                    push(
                        cbuf.at[tap, :, x_at(step)],
                        c1.at[tap, step - 1],
                        dp=y * SIDE + x_at(step),
                    )
                )
            else:
                copies.append(
                    push(
                        cbuf.at[tap, y_at(step)],
                        c1.at[tap, step - 1],
                        dp=y_at(step) * SIDE + x,
                    )
                )
        conv_first.append(copies)

    for copy in out_first:
        copy.wait_recv()
    total = obuf[y].astype(f32)
    for step in range(1, SIDE):
        total = total + o1[step - 1].astype(f32)
    o2[...] = total.astype(bf16)
    out_second = [
        push(o2.at[x_at(step)], o3.at[step - 1], dp=y * SIDE + x_at(step))
        for step in range(1, SIDE)
    ]

    grad_normed = jnp.zeros((ROWS, C), f32)
    conv_second = []
    for tap in range(TAPS):
        start = pl.multiple_of(s * ROWS + 2 * EDGE - tap * STEP, STEP)
        grad_normed = grad_normed + dot_nt(gall[pl.ds(start, ROWS)], w[tap])
        for copy in conv_first[tap]:
            copy.wait_recv()
        own = cbuf[tap, :, x] if tap % 2 == 0 else cbuf[tap, y]
        total = own.astype(f32)
        for step in range(1, SIDE):
            total = total + c1[tap, step - 1].astype(f32)
        c2[tap] = total.astype(bf16)
        copies = []
        for step in range(1, SIDE):
            if tap % 2 == 0:
                copies.append(
                    push(
                        c2.at[tap, y_at(step)],
                        c3.at[tap, step - 1],
                        dp=y_at(step) * SIDE + x,
                    )
                )
            else:
                copies.append(
                    push(
                        c2.at[tap, x_at(step)],
                        c3.at[tap, step - 1],
                        dp=y * SIDE + x_at(step),
                    )
                )
        conv_second.append(copies)

    for copy in out_second:
        copy.wait_recv()
    total = o2[x].astype(f32)
    for step in range(1, SIDE):
        total = total + o3[step - 1].astype(f32)
    oz[...] = total.astype(bf16)
    out_third = [
        push(oz, ozr.at[step - 1], seq=seq_at(2 * step)) for step in range(1, SIDE)
    ]

    for copy in block_slots:
        copy.wait_recv()
    act_float = act[...].astype(f32)
    upstream = (cot[...].astype(f32) + placed(brecv)).astype(bf16)
    spread = jnp.mean(grad_normed * act_float, axis=-1, keepdims=True)
    result[...] = (
        upstream.astype(f32)
        + inverse * grad_normed
        - inverse * inverse * inverse * act_float * spread
    ).astype(bf16)
    input_store = pltpu.make_async_copy(result, input_hbm.at[0], lsem.at[9])
    input_store.start()

    for tap in range(TAPS):
        for copy in conv_second[tap]:
            copy.wait_recv()
        total = (c2[tap, y] if tap % 2 == 0 else c2[tap, x]).astype(f32)
        for step in range(1, SIDE):
            total = total + c3[tap, step - 1].astype(f32)
        cout[tap] = total[:OWNED]
    conv_store = pltpu.make_async_copy(cout, conv_hbm, lsem.at[10])
    conv_store.start()

    for copy in out_third:
        copy.wait_recv()
    total = oz[...].astype(f32)
    for step in range(1, SIDE):
        total = total + ozr[step - 1].astype(f32)
    rows = total[0:3]
    for level in range(1, SIDE):
        rows = jnp.where(z == level, total[3 * level : 3 * level + 3], rows)
    oout[...] = rows
    out_store = pltpu.make_async_copy(oout, out_hbm, lsem.at[11])
    out_store.start()

    for copy in pending:
        copy.wait_send()
    for store in (block_store, input_store, conv_store, out_store):
        store.wait()


COPIES = 2 + 7 + 7 + 7 + 7 + 3 + 4 + 1 + 3 + 15 + 3 + 15 + 3


def shards(act, w, ow, cot, don, acc, flag, grad):
    any_space = pl.BlockSpec(memory_space=pl.ANY)
    vmem = pltpu.VMEM
    return pl.pallas_call(
        kernel,
        name="block_step",
        out_shape=(
            jax.ShapeDtypeStruct((1, ROWS, C), bf16),
            jax.ShapeDtypeStruct((1, ROWS, C), bf16),
            jax.ShapeDtypeStruct((TAPS, OWNED, M), f32),
            jax.ShapeDtypeStruct((3, C), f32),
        ),
        in_specs=[any_space] * 8,
        out_specs=[any_space] * 4,
        scratch_shapes=[
            vmem((ROWS, C), bf16),
            vmem((TAPS, C, M), bf16),
            vmem((M, C), bf16),
            vmem((ROWS, C), bf16),
            vmem((1, JUNC), i32),
            vmem((1, JUNC), i32),
            vmem((1, JUNC), i32),
            vmem((1, JUNC), f32),
            vmem((ROWS + 2 * EDGE, C), bf16),
            vmem((SEQ, ROWS, DP * BAND), bf16),
            vmem((LENGTH, DP * BAND), bf16),
            vmem((SLOTS, M), bf16),
            vmem((SLOTS, M), bf16),
            vmem((SLOTS, M), bf16),
            vmem((SLOTS, M), bf16),
            vmem((SLOTS, C), bf16),
            vmem((SLOTS, C), bf16),
            vmem((LENGTH + 2 * EDGE, M), bf16),
            vmem((TAPS, SIDE, SIDE, BAND, M), bf16),
            vmem((TAPS, SIDE - 1, SIDE, BAND, M), bf16),
            vmem((TAPS, SIDE, BAND, M), bf16),
            vmem((TAPS, SIDE - 1, BAND, M), bf16),
            vmem((2, SIDE, SIDE, BAND, C), bf16),
            vmem((SIDE, SIDE, BAND, C), bf16),
            vmem((SIDE, SIDE, BAND, C), bf16),
            vmem((SIDE - 1, SIDE, BAND, C), bf16),
            vmem((SIDE, BAND, C), bf16),
            vmem((SIDE - 1, BAND, C), bf16),
            vmem((BAND, C), bf16),
            vmem((SIDE - 1, BAND, C), bf16),
            vmem((ROWS, C), bf16),
            vmem((ROWS, C), bf16),
            vmem((TAPS, OWNED, M), f32),
            vmem((3, C), f32),
            pltpu.SemaphoreType.DMA((12,)),
            pltpu.SemaphoreType.DMA((COPIES,)),
            pltpu.SemaphoreType.DMA((COPIES,)),
        ],
        compiler_params=pltpu.CompilerParams(
            collective_id=0, has_side_effects=True, vmem_limit_bytes=56 * 1024 * 1024
        ),
    )(act, w, ow, cot, don, acc, flag, grad)


def solution(mesh):
    in_specs = (
        P("dp", "seq", None),
        P(),
        P(),
        P("dp", "seq", None),
        P("dp", None),
        P("dp", None),
        P("dp", None),
        P("dp", None),
    )
    out_specs = (
        P("dp", "seq", None),
        P("dp", "seq", None),
        P(None, ("dp", "seq"), None),
        P(("dp", "seq"), None),
    )
    return jax.shard_map(shards, mesh=mesh, in_specs=in_specs, out_specs=out_specs, check_vma=False)
```

```python
import itertools

import jax
import jax.numpy as jnp
from jax import lax
from jax.experimental import pallas as pl
from jax.experimental.pallas import tpu as pltpu
from jax.sharding import PartitionSpec as P

C = 1536
M = 384
TAPS = 5
STEP = 32
ROWS = 128
SEQ = 8
LENGTH = ROWS * SEQ
EDGE = TAPS // 2 * STEP
CAP = 16
JUNC = 448
PAIR = 2 * CAP
SLOTS = SEQ * PAIR
SIDE = 4
DP = SIDE * SIDE
OWNED = 12
BAND = 16
SHARE = DP * OWNED
YPART = 1024

TAP_ORDER = (0, 1, 4, 3, 2)
NEAR = (1, 7, 2, 6, 3, 5, 4)
X_EARLY = 7

EPS = 1e-06
SLOPE = 0.7978845608028654
CUBIC = 0.044715

MESH = pl.DeviceIdType.MESH
bf16 = jnp.bfloat16
f32 = jnp.float32
i32 = jnp.int32


def dot(a, b):
    return jnp.dot(a, b, preferred_element_type=f32)


def dot_nt(a, b):
    return lax.dot_general(a, b, (((1,), (1,)), ((), ())), preferred_element_type=f32)


def dot_tn(a, b):
    return lax.dot_general(a, b, (((0,), (0,)), ((), ())), preferred_element_type=f32)


def one_hot(count, row):
    return lax.broadcasted_iota(i32, (count, row.shape[1]), 0) == row


def ones_of(mask):
    return jnp.where(mask, 1.0, 0.0).astype(bf16)


def gelu_parts(v):
    curved = jnp.tanh(SLOPE * (v + CUBIC * v * v * v))
    hidden = 0.5 * v * (1.0 + curved)
    slope = 0.5 * (1.0 + curved) + 0.5 * v * (1.0 - curved * curved) * SLOPE * (
        1.0 + 3.0 * CUBIC * v * v
    )
    return hidden, slope


def junction_matrices(s, don, acc, flags, grad):
    scaled = grad * flags.astype(f32) * C ** (-0.5)
    high = scaled.astype(bf16)
    low = (scaled - high.astype(f32)).astype(bf16)
    don_owner = don >> 7
    acc_owner = acc >> 7
    pairs = ones_of(one_hot(SEQ * SEQ, don_owner * SEQ + acc_owner))
    earlier = ones_of(
        lax.broadcasted_iota(i32, (JUNC, JUNC), 0) < lax.broadcasted_iota(i32, (JUNC, JUNC), 1)
    )
    counts = dot(pairs, earlier)
    rank = jnp.sum(pairs.astype(f32) * counts, axis=0, keepdims=True).astype(i32)
    don_here = don_owner == s
    acc_here = acc_owner == s
    don_at = one_hot(ROWS, don - s * ROWS)
    acc_at = one_hot(ROWS, acc - s * ROWS)
    send_don = ones_of(one_hot(SLOTS, jnp.where(don_here, acc_owner * PAIR + rank, -1)))
    send_acc = ones_of(one_hot(SLOTS, jnp.where(acc_here, don_owner * PAIR + CAP + rank, -1)))
    select = (dot_nt(send_don, ones_of(don_at)) + dot_nt(send_acc, ones_of(acc_at))).astype(bf16)
    came_don = ones_of(one_hot(SLOTS, jnp.where(acc_here, don_owner * PAIR + rank, -1)))
    came_acc = ones_of(one_hot(SLOTS, jnp.where(don_here, acc_owner * PAIR + CAP + rank, -1)))

    def placing(weight):
        wide = weight.astype(f32)
        at_acc = jnp.where(acc_at, wide, 0.0).astype(bf16)
        at_don = jnp.where(don_at, wide, 0.0).astype(bf16)
        return (dot_nt(at_acc, came_don) + dot_nt(at_don, came_acc)).astype(bf16)

    return select, placing(high), placing(low)


def kernel(
    act_hbm,
    w_hbm,
    ow_hbm,
    cot_hbm,
    don_hbm,
    acc_hbm,
    flag_hbm,
    grad_hbm,
    block_hbm,
    input_hbm,
    conv_hbm,
    out_hbm,
    act,
    w,
    ow,
    cot,
    don,
    acc,
    flag,
    grad,
    edge_send,
    edge_recv,
    xsend,
    xall,
    xy_order,
    xx_order,
    gsend,
    grecv,
    hsend,
    hrecv,
    bsend,
    brecv,
    gall,
    cbuf,
    c1,
    c2,
    c3,
    osend_y,
    osend_x,
    osib_y,
    osib_x,
    obuf_y,
    obuf_x,
    o1_y,
    o1_x,
    o2_y,
    o2_x,
    o3_y,
    o3_x,
    oz,
    ozr,
    block,
    result,
    cout,
    oout,
    lsem,
    ssem,
    rsem,
):
    s = lax.axis_index("seq")
    d = lax.axis_index("dp")
    z, core = s // 2, s % 2
    y, x = d // SIDE, d % SIDE
    sibling = s + 1 - 2 * core
    ids = itertools.count()
    pending = []

    def push(src, dst, **device):
        i = next(ids)
        copy = pltpu.make_async_remote_copy(
            src_ref=src,
            dst_ref=dst,
            send_sem=ssem.at[i],
            recv_sem=rsem.at[i],
            device_id=device,
            device_id_type=MESH,
        )
        copy.start()
        pending.append(copy)
        return copy

    def seq_at(step):
        return lax.rem(s + step, SEQ)

    def x_at(step):
        return lax.rem(x + step, SIDE)

    def y_at(step):
        return lax.rem(y + step, SIDE)

    loads = {}
    for i, (name, src, dst) in enumerate(
        (
            ("act", act_hbm.at[0], act),
            ("don", don_hbm, don),
            ("acc", acc_hbm, acc),
            ("flag", flag_hbm, flag),
            ("grad", grad_hbm, grad),
            *((f"w{tap}", w_hbm.at[tap], w.at[tap]) for tap in TAP_ORDER),
            ("ow", ow_hbm, ow),
            ("cot", cot_hbm.at[0], cot),
        )
    ):
        loads[name] = pltpu.make_async_copy(src, dst, lsem.at[i])
        loads[name].start()

    barrier = pltpu.get_barrier_semaphore()
    for step in range(1, SEQ):
        pl.semaphore_signal(barrier, inc=1, device_id={"seq": seq_at(step)}, device_id_type=MESH)
    for step in range(1, SIDE):
        pl.semaphore_signal(
            barrier, inc=1, device_id={"dp": y * SIDE + x_at(step)}, device_id_type=MESH
        )
        pl.semaphore_signal(
            barrier, inc=1, device_id={"dp": y_at(step) * SIDE + x}, device_id_type=MESH
        )

    gall[0:EDGE] = jnp.zeros((EDGE, M), bf16)
    gall[EDGE + LENGTH :] = jnp.zeros((EDGE, M), bf16)

    loads["act"].wait()
    act_float = act[...].astype(f32)
    inverse = lax.rsqrt(jnp.mean(act_float * act_float, axis=-1, keepdims=True) + EPS)
    normed = (act_float * inverse).astype(bf16)

    column = lax.broadcasted_iota(i32, (1, C), 1)
    owner, lane = column // SHARE, column % SHARE
    regroup = ones_of(one_hot(C, lane // OWNED * (OWNED * SEQ) + owner * OWNED + lane % OWNED))
    grouped = dot(normed, regroup)
    left = lax.broadcasted_iota(i32, (ROWS // 2, 2 * SHARE), 1) < SHARE
    for pair in range(SEQ // 2):
        both = grouped[:, pair * 2 * SHARE : (pair + 1) * 2 * SHARE]
        upper, lower = both[: ROWS // 2], both[ROWS // 2 :]
        xsend[2 * pair] = jnp.where(left, upper, pltpu.roll(lower, SHARE, 1)).astype(bf16)
        xsend[2 * pair + 1] = jnp.where(left, pltpu.roll(upper, SHARE, 1), lower).astype(bf16)
    xall[s] = xsend[s]
    pl.semaphore_wait(barrier, SEQ - 1 + 2 * (SIDE - 1))

    def send_channels(steps):
        return [push(xsend.at[seq_at(step)], xall.at[s], seq=seq_at(step)) for step in steps]

    x_copies = send_channels(NEAR[:X_EARLY])

    taps = {}
    for tap in (0, 1):
        loads[f"w{tap}"].wait()
        taps[tap] = dot(normed, w[tap])
    half = ROWS // 2
    edge_send[0] = (
        taps[0][half:] + jnp.concatenate([taps[1][ROWS - STEP :], jnp.zeros((STEP, M), f32)], axis=0)
    ).astype(bf16)
    ahead = push(edge_send.at[0], edge_recv.at[0], seq=seq_at(1))
    for tap in (4, 3):
        loads[f"w{tap}"].wait()
        taps[tap] = dot(normed, w[tap])
    edge_send[1] = (
        taps[4][:half] + jnp.concatenate([jnp.zeros((STEP, M), f32), taps[3][:STEP]], axis=0)
    ).astype(bf16)
    behind = push(edge_send.at[1], edge_recv.at[1], seq=seq_at(SEQ - 1))
    for name in ("don", "acc", "flag", "grad"):
        loads[name].wait()
    select, place_high, place_low = junction_matrices(s, don[...], acc[...], flag[...], grad[...])

    def own_block(ref):
        return ref.at[pl.ds(pl.multiple_of(s * PAIR, PAIR), PAIR)]

    def send_slots(rows, out, into):
        out[...] = dot(select, rows).astype(bf16)
        own_block(into)[...] = own_block(out)[...]
        copies = []
        for step in NEAR:
            peer = seq_at(step)
            src = out.at[pl.ds(pl.multiple_of(peer * PAIR, PAIR), PAIR)]
            copies.append(push(src, own_block(into), seq=peer))
        return copies

    def placed(ref):
        return dot(place_high, ref[...]) + dot(place_low, ref[...])

    loads["ow"].wait()
    ow_value = ow[...]
    act_back = dot_nt(act[...], ow_value).astype(bf16)
    act_slots = send_slots(act_back, gsend, grecv)

    loads["w2"].wait()
    preact = dot(normed, w[2])
    preact = preact + jnp.concatenate(
        [
            taps[4][half:] + taps[3][STEP : STEP + half],
            jnp.concatenate([taps[3][STEP + half :], jnp.zeros((STEP, M), f32)], axis=0)
            + taps[0][:half]
            + taps[1][STEP : STEP + half],
        ],
        axis=0,
    )
    preact = preact + jnp.concatenate(
        [
            jnp.zeros((STEP, M), f32),
            taps[1][:STEP],
            jnp.zeros((half, M), f32),
        ],
        axis=0,
    )
    ahead.wait_recv()
    behind.wait_recv()
    preact = preact + jnp.concatenate(
        [
            jnp.where(s > 0, edge_recv[0].astype(f32), 0.0),
            jnp.where(s < SEQ - 1, edge_recv[1].astype(f32), 0.0),
        ],
        axis=0,
    )
    hidden_float, slope = gelu_parts(preact)
    hidden = hidden_float.astype(bf16)
    hidden_slots = send_slots(hidden, hsend, hrecv)

    x_copies += send_channels(NEAR[X_EARLY:])

    block[...] = (act[...].astype(f32) + dot(hidden, ow_value)).astype(bf16)
    block_store = pltpu.make_async_copy(block, block_hbm.at[0], lsem.at[12])
    block_store.start()
    loads["cot"].wait()
    cot_back = dot_nt(cot[...], ow_value)
    ow_square = dot_nt(ow_value, ow_value).astype(bf16)

    for copy in act_slots:
        copy.wait_recv()
    cot_back = cot_back + placed(grecv)
    for copy in hidden_slots:
        copy.wait_recv()
    mixed = placed(hrecv).astype(bf16)
    grad_hidden = cot_back + dot(mixed, ow_square)
    grad_here = pl.ds(pl.multiple_of(EDGE + s * ROWS, EDGE), ROWS)
    gall[grad_here] = (grad_hidden * slope).astype(bf16)

    def chunk(owner):
        return gall.at[pl.ds(pl.multiple_of(EDGE + owner * ROWS, EDGE), ROWS)]

    along = [push(chunk(s), chunk(s), seq=seq_at(2 * step)) for step in (1, 3, 2)]
    across = [push(chunk(s), chunk(s), seq=sibling)]

    def ordered(first):
        lane = lax.broadcasted_iota(i32, (1, M), 1)
        half, rest = lane // (DP * OWNED), lane % (DP * OWNED)
        outer, rest = rest // (SIDE * OWNED), rest % (SIDE * OWNED)
        inner, rest = rest // OWNED, rest % OWNED
        device = outer * SIDE + inner if first == "y" else inner * SIDE + outer
        order = ones_of(one_hot(M, device * 3 * SEQ + rest // 3 * 6 + half * 3 + rest % 3))
        return dot(hidden, order).astype(bf16), dot(mixed, order).astype(bf16)

    def out_terms(first, columns):
        hidden_order, mixed_order = ordered(first)
        terms = dot_tn(hidden_order, cot[:, columns]) + dot_tn(mixed_order, block[:, columns])
        return terms.astype(bf16).reshape(2, SIDE, SIDE * OWNED, columns.stop - columns.start)

    osend_y[...] = out_terms("y", slice(0, YPART))
    osend_x[...] = out_terms("x", slice(YPART, C))
    to_sibling = [
        push(osend_y.at[1 - core], osib_y, seq=sibling),
        push(osend_x.at[1 - core], osib_x, seq=sibling),
    ]

    for copy in to_sibling:
        copy.wait_recv()
    obuf_y[...] = (osend_y[core].astype(f32) + osib_y[...].astype(f32)).astype(bf16)
    obuf_x[...] = (osend_x[core].astype(f32) + osib_x[...].astype(f32)).astype(bf16)
    out_first = []
    for step in range(1, SIDE):
        out_first.append(push(obuf_y.at[y_at(step)], o1_y.at[step - 1], dp=y_at(step) * SIDE + x))
        out_first.append(push(obuf_x.at[x_at(step)], o1_x.at[step - 1], dp=y * SIDE + x_at(step)))

    for step, copy in zip((1, 3, 2), along):
        copy.wait_recv()
        owner = lax.rem(s + SEQ - 2 * step, SEQ)
        across.append(push(chunk(owner), chunk(owner), seq=sibling))

    block_slots = send_slots(block[...], bsend, brecv)

    def channels(first):
        lane = lax.broadcasted_iota(i32, (1, SHARE), 1)
        outer, rest = lane // (SIDE * OWNED), lane % (SIDE * OWNED)
        inner, row = rest // OWNED, rest % OWNED
        device = outer * SIDE + inner if first == "y" else inner * SIDE + outer
        parts = [
            dot(came, ones_of(one_hot(2 * SHARE, device * OWNED + row + SHARE * lower)))
            for lower in range(2)
        ]
        parts = [part.astype(bf16).reshape(SEQ, ROWS // 2, SHARE) for part in parts]
        return jnp.concatenate(parts, axis=1).reshape(LENGTH, SHARE)

    for copy in x_copies:
        copy.wait_recv()
    came = xall[...].reshape(SEQ * ROWS // 2, 2 * SHARE)
    xy_order[...] = channels("y")
    xx_order[...] = channels("x")

    for copy in across:
        copy.wait_recv()

    conv_first = []
    for tap in range(TAPS):
        start = 2 * EDGE - tap * STEP
        order = xx_order if tap % 2 == 0 else xy_order
        term = dot_tn(order[...], gall[start : start + LENGTH])
        cbuf[tap] = term.astype(bf16).reshape(SIDE, SIDE * OWNED, M)
        copies = []
        for step in range(1, SIDE):
            if tap % 2 == 0:
                at, peer = x_at(step), y * SIDE + x_at(step)
            else:
                at, peer = y_at(step), y_at(step) * SIDE + x
            copies.append(push(cbuf.at[tap, at], c1.at[tap, step - 1], dp=peer))
        conv_first.append(copies)

    band = lax.broadcasted_iota(i32, (SIDE * BAND, SIDE * OWNED), 0)
    packed = lax.broadcasted_iota(i32, (SIDE * BAND, SIDE * OWNED), 1)
    spread_rows = ones_of((band // BAND * OWNED + band % BAND == packed) & (band % BAND < OWNED))

    def summed(own, came):
        total = own.astype(f32)
        for step in range(1, SIDE):
            total = total + came[step - 1].astype(f32)
        return total

    def banded(total):
        bands = dot(spread_rows, total.astype(bf16)).astype(bf16)
        return bands.reshape(SIDE, BAND, total.shape[1])

    for copy in out_first:
        copy.wait_recv()
    o2_y[...] = banded(summed(obuf_y[y], o1_y))
    o2_x[...] = banded(summed(obuf_x[x], o1_x))
    out_second = []
    for step in range(1, SIDE):
        out_second.append(push(o2_y.at[x_at(step)], o3_y.at[step - 1], dp=y * SIDE + x_at(step)))
        out_second.append(push(o2_x.at[y_at(step)], o3_x.at[step - 1], dp=y_at(step) * SIDE + x))

    grad_normed = jnp.zeros((ROWS, C), f32)
    conv_second = []
    for tap in range(TAPS):
        start = pl.multiple_of(s * ROWS + 2 * EDGE - tap * STEP, STEP)
        grad_normed = grad_normed + dot_nt(gall[pl.ds(start, ROWS)], w[tap])
        for copy in conv_first[tap]:
            copy.wait_recv()
        own = cbuf[tap, x] if tap % 2 == 0 else cbuf[tap, y]
        c2[tap] = banded(summed(own, c1.at[tap]))
        copies = []
        for step in range(1, SIDE):
            if tap % 2 == 0:
                at, peer = y_at(step), y_at(step) * SIDE + x
            else:
                at, peer = x_at(step), y * SIDE + x_at(step)
            copies.append(push(c2.at[tap, at], c3.at[tap, step - 1], dp=peer))
        conv_second.append(copies)

    for copy in out_second:
        copy.wait_recv()
    oz[:, :YPART] = summed(o2_y[x], o3_y).astype(bf16)
    oz[:, YPART:] = summed(o2_x[y], o3_x).astype(bf16)
    out_third = [
        push(oz, ozr.at[step - 1], seq=seq_at(2 * step)) for step in range(1, SIDE)
    ]

    for copy in block_slots:
        copy.wait_recv()
    act_float = act[...].astype(f32)
    upstream = (cot[...].astype(f32) + placed(brecv)).astype(bf16)
    spread = jnp.mean(grad_normed * act_float, axis=-1, keepdims=True)
    result[...] = (
        upstream.astype(f32)
        + inverse * grad_normed
        - inverse * inverse * inverse * act_float * spread
    ).astype(bf16)
    input_store = pltpu.make_async_copy(result, input_hbm.at[0], lsem.at[13])
    input_store.start()

    for tap in range(TAPS):
        for copy in conv_second[tap]:
            copy.wait_recv()
        total = summed(c2[tap, y] if tap % 2 == 0 else c2[tap, x], c3.at[tap])
        cout[tap] = total[:OWNED]
    conv_store = pltpu.make_async_copy(cout, conv_hbm, lsem.at[14])
    conv_store.start()

    for copy in out_third:
        copy.wait_recv()
    total = summed(oz[...], ozr)
    rows = total[0:3]
    for level in range(1, SIDE):
        rows = jnp.where(z == level, total[3 * level : 3 * level + 3], rows)
    oout[...] = rows
    out_store = pltpu.make_async_copy(oout, out_hbm, lsem.at[15])
    out_store.start()

    for copy in pending:
        copy.wait_send()
    for store in (block_store, input_store, conv_store, out_store):
        store.wait()


COPIES = 2 + 7 + 7 + 7 + 7 + 3 + 4 + 2 + 6 + 15 + 6 + 15 + 3


def store_kernel(*refs):
    came, left, held, sem = refs[:4], refs[4:8], refs[8:12], refs[12]
    loads = [pltpu.make_async_copy(came[i], held[i], sem.at[i]) for i in range(4)]
    stores = [pltpu.make_async_copy(held[i], left[i], sem.at[4 + i]) for i in range(4)]
    for load in loads:
        load.start()
    for load, store in zip(loads, stores):
        load.wait()
        store.start()
    for store in stores:
        store.wait()


OUTPUTS = (
    jax.ShapeDtypeStruct((1, ROWS, C), bf16),
    jax.ShapeDtypeStruct((1, ROWS, C), bf16),
    jax.ShapeDtypeStruct((TAPS, OWNED, M), f32),
    jax.ShapeDtypeStruct((3, C), f32),
)


def shards(act, w, ow, cot, don, acc, flag, grad):
    any_space = pl.BlockSpec(memory_space=pl.ANY)
    vmem = pltpu.VMEM
    results = pl.pallas_call(
        kernel,
        name="block_step",
        out_shape=OUTPUTS,
        in_specs=[any_space] * 8,
        out_specs=[any_space] * 4,
        scratch_shapes=[
            vmem((ROWS, C), bf16),
            vmem((TAPS, C, M), bf16),
            vmem((M, C), bf16),
            vmem((ROWS, C), bf16),
            vmem((1, JUNC), i32),
            vmem((1, JUNC), i32),
            vmem((1, JUNC), i32),
            vmem((1, JUNC), f32),
            vmem((2, EDGE, M), bf16),
            vmem((2, EDGE, M), bf16),
            vmem((SEQ, ROWS // 2, 2 * SHARE), bf16),
            vmem((SEQ, ROWS // 2, 2 * SHARE), bf16),
            vmem((LENGTH, SHARE), bf16),
            vmem((LENGTH, SHARE), bf16),
            vmem((SLOTS, M), bf16),
            vmem((SLOTS, M), bf16),
            vmem((SLOTS, M), bf16),
            vmem((SLOTS, M), bf16),
            vmem((SLOTS, C), bf16),
            vmem((SLOTS, C), bf16),
            vmem((LENGTH + 2 * EDGE, M), bf16),
            vmem((TAPS, SIDE, SIDE * OWNED, M), bf16),
            vmem((TAPS, SIDE - 1, SIDE * OWNED, M), bf16),
            vmem((TAPS, SIDE, BAND, M), bf16),
            vmem((TAPS, SIDE - 1, BAND, M), bf16),
            vmem((2, SIDE, SIDE * OWNED, YPART), bf16),
            vmem((2, SIDE, SIDE * OWNED, C - YPART), bf16),
            vmem((SIDE, SIDE * OWNED, YPART), bf16),
            vmem((SIDE, SIDE * OWNED, C - YPART), bf16),
            vmem((SIDE, SIDE * OWNED, YPART), bf16),
            vmem((SIDE, SIDE * OWNED, C - YPART), bf16),
            vmem((SIDE - 1, SIDE * OWNED, YPART), bf16),
            vmem((SIDE - 1, SIDE * OWNED, C - YPART), bf16),
            vmem((SIDE, BAND, YPART), bf16),
            vmem((SIDE, BAND, C - YPART), bf16),
            vmem((SIDE - 1, BAND, YPART), bf16),
            vmem((SIDE - 1, BAND, C - YPART), bf16),
            vmem((BAND, C), bf16),
            vmem((SIDE - 1, BAND, C), bf16),
            vmem((ROWS, C), bf16),
            vmem((ROWS, C), bf16),
            vmem((TAPS, OWNED, M), f32),
            vmem((3, C), f32),
            pltpu.SemaphoreType.DMA((16,)),
            pltpu.SemaphoreType.DMA((COPIES,)),
            pltpu.SemaphoreType.DMA((COPIES,)),
        ],
        compiler_params=pltpu.CompilerParams(
            collective_id=0, has_side_effects=True, vmem_limit_bytes=56 * 1024 * 1024
        ),
    )(act, w, ow, cot, don, acc, flag, grad)
    return pl.pallas_call(
        store_kernel,
        name="store_results",
        out_shape=OUTPUTS,
        in_specs=[any_space] * 4,
        out_specs=[any_space] * 4,
        scratch_shapes=[
            *(vmem(out.shape, out.dtype) for out in OUTPUTS),
            pltpu.SemaphoreType.DMA((8,)),
        ],
    )(*results)


def solution(mesh):
    in_specs = (
        P("dp", "seq", None),
        P(),
        P(),
        P("dp", "seq", None),
        P("dp", None),
        P("dp", None),
        P("dp", None),
        P("dp", None),
    )
    out_specs = (
        P("dp", "seq", None),
        P("dp", "seq", None),
        P(None, ("dp", "seq"), None),
        P(("dp", "seq"), None),
    )
    return jax.shard_map(shards, mesh=mesh, in_specs=in_specs, out_specs=out_specs, check_vma=False)
```

```python
import itertools

import jax
import jax.numpy as jnp
from jax import lax
from jax.experimental import pallas as pl
from jax.experimental.pallas import tpu as pltpu
from jax.sharding import PartitionSpec as P

C = 1536
M = 384
TAPS = 5
STEP = 32
ROWS = 128
SEQ = 8
LENGTH = ROWS * SEQ
EDGE = TAPS // 2 * STEP
CAP = 16
JUNC = 448
PAIR = 2 * CAP
SLOTS = SEQ * PAIR
SIDE = 4
DP = SIDE * SIDE
OWNED = 12
BAND = 16
SHARE = DP * OWNED
YPART = 1024
PARTS = (slice(0, 128), slice(128, M))
WIDTHS = tuple(part.stop - part.start for part in PARTS)
UNITS = ((0, (0, 2), "z"), (0, (1, 3, 4), "y"), (1, (1, 3), "y"), (1, (0, 2, 4), "z"))
SIZES = tuple((len(taps), WIDTHS[part]) for part, taps, _ in UNITS)

TAP_ORDER = (0, 1, 4, 3, 2)
FAR = (4, 3, 5, 2, 6, 1, 7)

EPS = 1e-06
SLOPE = 0.7978845608028654
CUBIC = 0.044715

MESH = pl.DeviceIdType.MESH
bf16 = jnp.bfloat16
f32 = jnp.float32
i32 = jnp.int32


def dot(a, b):
    return jnp.dot(a, b, preferred_element_type=f32)


def dot_nt(a, b):
    return lax.dot_general(a, b, (((1,), (1,)), ((), ())), preferred_element_type=f32)


def dot_tn(a, b):
    return lax.dot_general(a, b, (((0,), (0,)), ((), ())), preferred_element_type=f32)


def one_hot(count, row):
    return lax.broadcasted_iota(i32, (count, row.shape[1]), 0) == row


def ones_of(mask):
    return jnp.where(mask, 1.0, 0.0).astype(bf16)


def gelu_parts(v):
    curved = jnp.tanh(SLOPE * (v + CUBIC * v * v * v))
    hidden = 0.5 * v * (1.0 + curved)
    slope = 0.5 * (1.0 + curved) + 0.5 * v * (1.0 - curved * curved) * SLOPE * (
        1.0 + 3.0 * CUBIC * v * v
    )
    return hidden, slope


def junction_matrices(s, don, acc, flags, grad):
    scaled = grad * flags.astype(f32) * C ** (-0.5)
    high = scaled.astype(bf16)
    low = (scaled - high.astype(f32)).astype(bf16)
    don_owner = don >> 7
    acc_owner = acc >> 7
    pairs = ones_of(one_hot(SEQ * SEQ, don_owner * SEQ + acc_owner))
    earlier = ones_of(
        lax.broadcasted_iota(i32, (JUNC, JUNC), 0) < lax.broadcasted_iota(i32, (JUNC, JUNC), 1)
    )
    counts = dot(pairs, earlier)
    rank = jnp.sum(pairs.astype(f32) * counts, axis=0, keepdims=True).astype(i32)
    don_here = don_owner == s
    acc_here = acc_owner == s
    don_at = one_hot(ROWS, don - s * ROWS)
    acc_at = one_hot(ROWS, acc - s * ROWS)
    send_don = ones_of(one_hot(SLOTS, jnp.where(don_here, acc_owner * PAIR + rank, -1)))
    send_acc = ones_of(one_hot(SLOTS, jnp.where(acc_here, don_owner * PAIR + CAP + rank, -1)))
    select = (dot_nt(send_don, ones_of(don_at)) + dot_nt(send_acc, ones_of(acc_at))).astype(bf16)
    came_don = ones_of(one_hot(SLOTS, jnp.where(acc_here, don_owner * PAIR + rank, -1)))
    came_acc = ones_of(one_hot(SLOTS, jnp.where(don_here, acc_owner * PAIR + CAP + rank, -1)))

    def placing(weight):
        wide = weight.astype(f32)
        at_acc = jnp.where(acc_at, wide, 0.0).astype(bf16)
        at_don = jnp.where(don_at, wide, 0.0).astype(bf16)
        return (dot_nt(at_acc, came_don) + dot_nt(at_don, came_acc)).astype(bf16)

    return select, placing(high), placing(low)


def kernel(
    act_hbm,
    w_hbm,
    ow_hbm,
    cot_hbm,
    don_hbm,
    acc_hbm,
    flag_hbm,
    grad_hbm,
    block,
    result,
    cout,
    oout,
    act,
    w,
    ow,
    cot,
    don,
    acc,
    flag,
    grad,
    edge_send,
    edge_recv,
    xsend,
    xall,
    xedge,
    xhalo,
    window_y,
    window_z,
    gsend,
    grecv,
    hsend,
    hrecv,
    bsend,
    brecv,
    gall,
    gpad,
    cbuf,
    c1,
    c2,
    c3,
    osend_y,
    osend_x,
    osib_y,
    osib_x,
    obuf_y,
    obuf_x,
    o1_y,
    o1_x,
    o2_y,
    o2_x,
    o3_y,
    o3_x,
    oz,
    ozr,
    lsem,
    ssem,
    rsem,
):
    s = lax.axis_index("seq")
    d = lax.axis_index("dp")
    z, core = s // 2, s % 2
    y, x = d // SIDE, d % SIDE
    sibling = s + 1 - 2 * core
    ids = itertools.count()
    pending = []

    def push(src, dst, **device):
        i = next(ids)
        copy = pltpu.make_async_remote_copy(
            src_ref=src,
            dst_ref=dst,
            send_sem=ssem.at[i],
            recv_sem=rsem.at[i],
            device_id=device,
            device_id_type=MESH,
        )
        copy.start()
        pending.append(copy)
        return copy

    def seq_at(step):
        return lax.rem(s + step, SEQ)

    def x_at(step):
        return lax.rem(x + step, SIDE)

    def y_at(step):
        return lax.rem(y + step, SIDE)

    def x_peer(step):
        return y * SIDE + x_at(step)

    def y_peer(step):
        return y_at(step) * SIDE + x

    def z_at(step):
        return lax.rem(z + step, SIDE)

    loads = {}
    for i, (name, src, dst) in enumerate(
        (
            ("act", act_hbm.at[0], act),
            ("don", don_hbm, don),
            ("acc", acc_hbm, acc),
            ("flag", flag_hbm, flag),
            ("grad", grad_hbm, grad),
            *((f"w{tap}", w_hbm.at[tap], w.at[tap]) for tap in TAP_ORDER),
            ("ow", ow_hbm, ow),
            ("cot", cot_hbm.at[0], cot),
        )
    ):
        loads[name] = pltpu.make_async_copy(src, dst, lsem.at[i])
        loads[name].start()

    barrier = pltpu.get_barrier_semaphore()
    for step in range(1, SEQ):
        pl.semaphore_signal(barrier, inc=1, device_id={"seq": seq_at(step)}, device_id_type=MESH)
    for step in range(1, SIDE):
        pl.semaphore_signal(barrier, inc=1, device_id={"dp": y_peer(step)}, device_id_type=MESH)
        pl.semaphore_signal(barrier, inc=1, device_id={"dp": x_peer(step)}, device_id_type=MESH)
        pl.semaphore_signal(
            barrier, inc=1, device_id={"dp": x_peer(step), "seq": sibling}, device_id_type=MESH
        )

    loads["act"].wait()
    act_float = act[...].astype(f32)
    inverse = lax.rsqrt(jnp.mean(act_float * act_float, axis=-1, keepdims=True) + EPS)
    normed = (act_float * inverse).astype(bf16)

    me = x * 2 + core
    column = lax.broadcasted_iota(i32, (1, C), 1)
    owner, lane = column // SHARE, column % SHARE
    device = lane // OWNED
    channel = (
        (device // SIDE * SIDE + owner // 2) * (OWNED * SEQ)
        + (device % SIDE * 2 + owner % 2) * OWNED
        + lane % OWNED
    )
    grouped = dot(normed, ones_of(one_hot(C, channel)))
    left = lax.broadcasted_iota(i32, (STEP, 2 * SHARE), 1) < SHARE
    for upper_lower in range(2):
        for pair in range(SEQ // 2):
            both = grouped[
                2 * upper_lower * STEP : 2 * (upper_lower + 1) * STEP, pair * 2 * SHARE : (pair + 1) * 2 * SHARE
            ]
            upper, lower = both[:STEP], both[STEP:]
            xsend[upper_lower, 2 * pair] = jnp.where(left, upper, pltpu.roll(lower, SHARE, 1)).astype(bf16)
            xsend[upper_lower, 2 * pair + 1] = jnp.where(left, pltpu.roll(upper, SHARE, 1), lower).astype(
                bf16
            )
    xall[me] = xsend[:, me]
    pl.semaphore_wait(barrier, SEQ - 1 + 3 * (SIDE - 1))

    row_peers = [
        (step, turn) for step in (2, 1, 3) for turn in range(2)
    ]

    def row_device(step, turn):
        seq = sibling if turn else s
        return x_at(step) * 2 + lax.rem(core + turn, 2), dict(dp=x_peer(step), seq=seq)

    x_copies = []
    for step, turn in row_peers:
        to, device_id = row_device(step, turn)
        x_copies.append(push(xsend.at[:, to], xall.at[me], **device_id))
    x_copies.append(push(xsend.at[:, x * 2 + 1 - core], xall.at[me], seq=sibling))
    outer = lax.rem(s + SEQ - 1 + 2 * core, SEQ)
    edge_rows = push(xsend.at[core], xedge, seq=outer)

    taps = {}
    for tap in (0, 1):
        loads[f"w{tap}"].wait()
        taps[tap] = dot(normed, w[tap])
    half = ROWS // 2
    edge_send[0] = (
        taps[0][half:] + jnp.concatenate([taps[1][ROWS - STEP :], jnp.zeros((STEP, M), f32)], axis=0)
    ).astype(bf16)
    ahead = push(edge_send.at[0], edge_recv.at[0], seq=seq_at(1))
    for tap in (4, 3):
        loads[f"w{tap}"].wait()
        taps[tap] = dot(normed, w[tap])
    edge_send[1] = (
        taps[4][:half] + jnp.concatenate([jnp.zeros((STEP, M), f32), taps[3][:STEP]], axis=0)
    ).astype(bf16)
    behind = push(edge_send.at[1], edge_recv.at[1], seq=seq_at(SEQ - 1))
    for name in ("don", "acc", "flag", "grad"):
        loads[name].wait()
    select, place_high, place_low = junction_matrices(s, don[...], acc[...], flag[...], grad[...])

    def own_block(ref):
        return ref.at[pl.ds(pl.multiple_of(s * PAIR, PAIR), PAIR)]

    def send_slots(rows, out, into):
        out[...] = dot(select, rows).astype(bf16)
        own_block(into)[...] = own_block(out)[...]
        copies = []
        for step in FAR:
            peer = seq_at(step)
            src = out.at[pl.ds(pl.multiple_of(peer * PAIR, PAIR), PAIR)]
            copies.append(push(src, own_block(into), seq=peer))
        return copies

    def placed(ref):
        return dot(place_high, ref[...]) + dot(place_low, ref[...])

    loads["ow"].wait()
    ow_value = ow[...]
    act_back = dot_nt(act[...], ow_value).astype(bf16)
    act_slots = send_slots(act_back, gsend, grecv)

    loads["w2"].wait()
    preact = dot(normed, w[2])
    preact = preact + jnp.concatenate(
        [
            taps[4][half:] + taps[3][STEP : STEP + half],
            jnp.concatenate([taps[3][STEP + half :], jnp.zeros((STEP, M), f32)], axis=0)
            + taps[0][:half]
            + taps[1][STEP : STEP + half],
        ],
        axis=0,
    )
    preact = preact + jnp.concatenate(
        [
            jnp.zeros((STEP, M), f32),
            taps[1][:STEP],
            jnp.zeros((half, M), f32),
        ],
        axis=0,
    )
    ahead.wait_recv()
    behind.wait_recv()
    preact = preact + jnp.concatenate(
        [
            jnp.where(s > 0, edge_recv[0].astype(f32), 0.0),
            jnp.where(s < SEQ - 1, edge_recv[1].astype(f32), 0.0),
        ],
        axis=0,
    )
    hidden_float, slope = gelu_parts(preact)
    hidden = hidden_float.astype(bf16)
    hidden_slots = send_slots(hidden, hsend, hrecv)

    edge_rows.wait_recv()
    xhalo[me] = xedge[me]
    for step, turn in row_peers:
        to, device_id = row_device(step, turn)
        x_copies.append(push(xedge.at[to], xhalo.at[me], **device_id))
    x_copies.append(push(xedge.at[x * 2 + 1 - core], xhalo.at[me], seq=sibling))

    block[0] = (act[...].astype(f32) + dot(hidden, ow_value)).astype(bf16)
    loads["cot"].wait()
    cot_back = dot_nt(cot[...], ow_value)
    ow_square = dot_nt(ow_value, ow_value).astype(bf16)

    for copy in act_slots:
        copy.wait_recv()
    cot_back = cot_back + placed(grecv)
    for copy in hidden_slots:
        copy.wait_recv()
    mixed = placed(hrecv).astype(bf16)
    grad_hidden = cot_back + dot(mixed, ow_square)
    grad_pre = (grad_hidden * slope).astype(bf16)
    own_rows = pl.ds(pl.multiple_of(me * ROWS, ROWS), ROWS)
    for part, columns in zip(gall, PARTS):
        part[own_rows] = grad_pre[:, columns]
    gpad[EDGE : EDGE + ROWS] = grad_pre

    def chunk(part, owner):
        return part.at[pl.ds(pl.multiple_of(owner * ROWS, ROWS), ROWS)]

    along, across = [], []

    def spread(part):
        along.append(
            [push(chunk(part, me), chunk(part, me), dp=x_peer(step)) for step in (2, 1, 3)]
        )
        across.append([push(chunk(part, me), chunk(part, me), seq=sibling)])

    def forward(i):
        for step, copy in ((1, along[i][1]), (3, along[i][2]), (2, along[i][0])):
            copy.wait_recv()
            owner = x_at(SIDE - step) * 2 + core
            across[i].append(push(chunk(gall[i], owner), chunk(gall[i], owner), seq=sibling))

    spread(gall[0])
    spread(gall[1])
    pad_copies = [
        push(gpad.at[ROWS : ROWS + EDGE], gpad.at[0:EDGE], seq=seq_at(1)),
        push(gpad.at[EDGE : 2 * EDGE], gpad.at[EDGE + ROWS :], seq=seq_at(SEQ - 1)),
    ]
    block_slots = send_slots(block[0], bsend, brecv)

    def ordered(first):
        lane = lax.broadcasted_iota(i32, (1, M), 1)
        half, rest = lane // (DP * OWNED), lane % (DP * OWNED)
        outer, rest = rest // (SIDE * OWNED), rest % (SIDE * OWNED)
        inner, rest = rest // OWNED, rest % OWNED
        device = outer * SIDE + inner if first == "y" else inner * SIDE + outer
        order = ones_of(one_hot(M, device * 3 * SEQ + rest // 3 * 6 + half * 3 + rest % 3))
        return dot(hidden, order).astype(bf16), dot(mixed, order).astype(bf16)

    def out_terms(first, columns):
        hidden_order, mixed_order = ordered(first)
        terms = dot_tn(hidden_order, cot[:, columns]) + dot_tn(mixed_order, block[0, :, columns])
        return terms.astype(bf16).reshape(2, SIDE, SIDE * OWNED, columns.stop - columns.start)

    osend_y[...] = out_terms("y", slice(0, YPART))
    osend_x[...] = out_terms("x", slice(YPART, C))
    to_sibling = [
        push(osend_y.at[1 - core], osib_y, seq=sibling),
        push(osend_x.at[1 - core], osib_x, seq=sibling),
    ]

    for copy in to_sibling:
        copy.wait_recv()
    obuf_y[...] = (osend_y[core].astype(f32) + osib_y[...].astype(f32)).astype(bf16)
    obuf_x[...] = (osend_x[core].astype(f32) + osib_x[...].astype(f32)).astype(bf16)
    out_first = []
    for step in range(1, SIDE):
        out_first.append(push(obuf_y.at[y_at(step)], o1_y.at[step - 1], dp=y_at(step) * SIDE + x))
        out_first.append(push(obuf_x.at[x_at(step)], o1_x.at[step - 1], dp=y * SIDE + x_at(step)))

    def unpacked(came, first):
        lane = lax.broadcasted_iota(i32, (1, SHARE), 1)
        outer, rest = lane // (SIDE * OWNED), lane % (SIDE * OWNED)
        inner, row = rest // OWNED, rest % OWNED
        device = outer * SIDE + inner if first == "y" else inner * SIDE + outer
        flat = came.reshape(-1, 2 * SHARE)
        parts = [
            dot(flat, ones_of(one_hot(2 * SHARE, device * OWNED + row + SHARE * lower)))
            for lower in range(2)
        ]
        parts = [part.astype(bf16).reshape(-1, STEP, SHARE) for part in parts]
        return jnp.concatenate(parts, axis=1)

    def windows(first):
        middle = unpacked(xall[...], first).reshape(SIDE, 2 * ROWS, SHARE)
        sides = unpacked(xhalo[...], first).reshape(SIDE, 2, EDGE, SHARE)
        nothing = jnp.zeros((SIDE, EDGE, SHARE), bf16)
        return jnp.concatenate(
            [
                jnp.where(z > 0, sides[:, 0], nothing),
                middle,
                jnp.where(z < SIDE - 1, sides[:, 1], nothing),
            ],
            axis=1,
        )

    for copy in x_copies:
        copy.wait_recv()
    window_y[...] = windows("y")
    window_z[...] = windows("z")

    def zy_device(axis, step):
        if axis == "z":
            return z_at(step), dict(seq=seq_at(2 * step))
        return y_at(step), dict(dp=y_peer(step))

    def conv_terms(u):
        part, taps_here, first = UNITS[u]
        window = window_z if first == "z" else window_y
        for i, tap in enumerate(taps_here):
            rows = window[:, tap * STEP : tap * STEP + 2 * ROWS].reshape(LENGTH, SHARE)
            term = dot_tn(rows, gall[part][...])
            cbuf[u][i] = term.astype(bf16).reshape(SIDE, SIDE * OWNED, term.shape[1])
        copies = []
        for step in (2, 1, 3):
            at, peer = zy_device(first, step)
            copies.append(push(cbuf[u].at[:, at], c1[u].at[step - 1], **peer))
        return copies

    forward(0)
    for copy in across[0]:
        copy.wait_recv()
    conv_first = [conv_terms(0)]
    forward(1)
    conv_first.append(conv_terms(1))
    for copy in across[1]:
        copy.wait_recv()
    conv_first.append(conv_terms(2))
    conv_first.append(conv_terms(3))

    band = lax.broadcasted_iota(i32, (SIDE * BAND, SIDE * OWNED), 0)
    packed = lax.broadcasted_iota(i32, (SIDE * BAND, SIDE * OWNED), 1)
    spread_rows = ones_of((band // BAND * OWNED + band % BAND == packed) & (band % BAND < OWNED))

    def summed(own, came):
        total = own.astype(f32)
        for step in range(1, SIDE):
            total = total + came[step - 1].astype(f32)
        return total

    def banded(total):
        bands = dot(spread_rows, total.astype(bf16)).astype(bf16)
        return bands.reshape(SIDE, BAND, total.shape[1])

    for copy in out_first:
        copy.wait_recv()
    o2_y[...] = banded(summed(obuf_y[y], o1_y))
    o2_x[...] = banded(summed(obuf_x[x], o1_x))
    out_second = []
    for step in range(1, SIDE):
        out_second.append(push(o2_y.at[x_at(step)], o3_y.at[step - 1], dp=y * SIDE + x_at(step)))
        out_second.append(push(o2_x.at[y_at(step)], o3_x.at[step - 1], dp=y_at(step) * SIDE + x))

    for copy in pad_copies:
        copy.wait_recv()

    @pl.when(s == 0)
    def _():
        gpad[0:EDGE] = jnp.zeros((EDGE, M), bf16)

    @pl.when(s == SEQ - 1)
    def _():
        gpad[EDGE + ROWS :] = jnp.zeros((EDGE, M), bf16)

    grad_normed = jnp.zeros((ROWS, C), f32)
    for tap in range(TAPS):
        start = 2 * EDGE - tap * STEP
        grad_normed = grad_normed + dot_nt(gpad[start : start + ROWS], w[tap])

    conv_second = []
    for u, (part, taps_here, first) in enumerate(UNITS):
        for copy in conv_first[u]:
            copy.wait_recv()
        mine = z if first == "z" else y
        for i in range(len(taps_here)):
            total = cbuf[u][i, mine].astype(f32)
            for step in range(1, SIDE):
                total = total + c1[u][step - 1, i].astype(f32)
            c2[u][:, i] = banded(total)
        copies = []
        for step in (2, 1, 3):
            at, peer = zy_device("y" if first == "z" else "z", step)
            copies.append(push(c2[u].at[at], c3[u].at[step - 1], **peer))
        conv_second.append(copies)

    for copy in out_second:
        copy.wait_recv()
    total = jnp.concatenate([summed(o2_y[x], o3_y), summed(o2_x[y], o3_x)], axis=1)
    for level in range(SIDE):
        mine = total[3 * level : 3 * (level + 1)]
        quarters = [mine[:, i * M : (i + 1) * M] for i in range(SIDE)]
        oz[level] = jnp.concatenate([*quarters, jnp.zeros((BAND - OWNED, M), f32)], axis=0).astype(
            bf16
        )
    out_third = [
        push(oz.at[z_at(step)], ozr.at[step - 1], seq=seq_at(2 * step)) for step in range(1, SIDE)
    ]

    for copy in block_slots:
        copy.wait_recv()
    act_float = act[...].astype(f32)
    upstream = (cot[...].astype(f32) + placed(brecv)).astype(bf16)
    spread = jnp.mean(grad_normed * act_float, axis=-1, keepdims=True)
    result[0] = (
        upstream.astype(f32)
        + inverse * grad_normed
        - inverse * inverse * inverse * act_float * spread
    ).astype(bf16)
    for u, (part, taps_here, first) in enumerate(UNITS):
        for copy in conv_second[u]:
            copy.wait_recv()
        mine = y if first == "z" else z
        for i, tap in enumerate(taps_here):
            total = summed(c2[u][mine, i], c3[u].at[:, i])
            cout[tap, :, PARTS[part]] = total[:OWNED]

    for copy in out_third:
        copy.wait_recv()
    total = summed(oz[z], ozr)
    rows = jnp.concatenate([total[3 * i : 3 * (i + 1)] for i in range(SIDE)], axis=1)
    oout[...] = rows
    for copy in pending:
        copy.wait_send()


COPIES = 2 + 7 + 8 + 7 + 7 + 7 + 2 * (3 + 4) + 2 + 2 + 6 + 12 + 6 + 12 + 3


def store_kernel(*refs):
    came, left, sem = refs[:4], refs[4:8], refs[8]
    stores = [pltpu.make_async_copy(came[i], left[i], sem.at[i]) for i in range(4)]
    for store in stores:
        store.start()
    for store in stores:
        store.wait()


OUTPUTS = (
    jax.ShapeDtypeStruct((1, ROWS, C), bf16),
    jax.ShapeDtypeStruct((1, ROWS, C), bf16),
    jax.ShapeDtypeStruct((TAPS, OWNED, M), f32),
    jax.ShapeDtypeStruct((3, C), f32),
)


def shards(act, w, ow, cot, don, acc, flag, grad):
    any_space = pl.BlockSpec(memory_space=pl.ANY)
    vmem = pltpu.VMEM
    results = pl.pallas_call(
        kernel,
        name="block_step",
        out_shape=tuple(vmem(o.shape, o.dtype) for o in OUTPUTS),
        in_specs=[pl.BlockSpec(memory_space=pltpu.HBM)] * 8,
        out_specs=[pl.BlockSpec(memory_space=vmem)] * 4,
        scratch_shapes=[
            vmem((ROWS, C), bf16),
            vmem((TAPS, C, M), bf16),
            vmem((M, C), bf16),
            vmem((ROWS, C), bf16),
            vmem((1, JUNC), i32),
            vmem((1, JUNC), i32),
            vmem((1, JUNC), i32),
            vmem((1, JUNC), f32),
            vmem((2, EDGE, M), bf16),
            vmem((2, EDGE, M), bf16),
            vmem((2, SEQ, STEP, 2 * SHARE), bf16),
            vmem((SEQ, 2, STEP, 2 * SHARE), bf16),
            vmem((SEQ, STEP, 2 * SHARE), bf16),
            vmem((SEQ, STEP, 2 * SHARE), bf16),
            vmem((SIDE, 2 * (ROWS + EDGE), SHARE), bf16),
            vmem((SIDE, 2 * (ROWS + EDGE), SHARE), bf16),
            vmem((SLOTS, M), bf16),
            vmem((SLOTS, M), bf16),
            vmem((SLOTS, M), bf16),
            vmem((SLOTS, M), bf16),
            vmem((SLOTS, C), bf16),
            vmem((SLOTS, C), bf16),
            [vmem((LENGTH, width), bf16) for width in WIDTHS],
            vmem((ROWS + 2 * EDGE, M), bf16),
            [vmem((n, SIDE, SIDE * OWNED, width), bf16) for n, width in SIZES],
            [vmem((SIDE - 1, n, SIDE * OWNED, width), bf16) for n, width in SIZES],
            [vmem((SIDE, n, BAND, width), bf16) for n, width in SIZES],
            [vmem((SIDE - 1, n, BAND, width), bf16) for n, width in SIZES],
            vmem((2, SIDE, SIDE * OWNED, YPART), bf16),
            vmem((2, SIDE, SIDE * OWNED, C - YPART), bf16),
            vmem((SIDE, SIDE * OWNED, YPART), bf16),
            vmem((SIDE, SIDE * OWNED, C - YPART), bf16),
            vmem((SIDE, SIDE * OWNED, YPART), bf16),
            vmem((SIDE, SIDE * OWNED, C - YPART), bf16),
            vmem((SIDE - 1, SIDE * OWNED, YPART), bf16),
            vmem((SIDE - 1, SIDE * OWNED, C - YPART), bf16),
            vmem((SIDE, BAND, YPART), bf16),
            vmem((SIDE, BAND, C - YPART), bf16),
            vmem((SIDE - 1, BAND, YPART), bf16),
            vmem((SIDE - 1, BAND, C - YPART), bf16),
            vmem((SIDE, BAND, M), bf16),
            vmem((SIDE - 1, BAND, M), bf16),
            pltpu.SemaphoreType.DMA((12,)),
            pltpu.SemaphoreType.DMA((COPIES,)),
            pltpu.SemaphoreType.DMA((COPIES,)),
        ],
        compiler_params=pltpu.CompilerParams(
            collective_id=0, has_side_effects=True, vmem_limit_bytes=56 * 1024 * 1024
        ),
    )(act, w, ow, cot, don, acc, flag, grad)
    return pl.pallas_call(
        store_kernel,
        name="store_results",
        out_shape=OUTPUTS,
        in_specs=[pl.BlockSpec(memory_space=vmem)] * 4,
        out_specs=[any_space] * 4,
        scratch_shapes=[pltpu.SemaphoreType.DMA((4,))],
    )(*(pltpu.with_memory_space_constraint(r, pltpu.VMEM) for r in results))


def solution(mesh):
    in_specs = (
        P("dp", "seq", None),
        P(),
        P(),
        P("dp", "seq", None),
        P("dp", None),
        P("dp", None),
        P("dp", None),
        P("dp", None),
    )
    out_specs = (
        P("dp", "seq", None),
        P("dp", "seq", None),
        P(None, ("dp", "seq"), None),
        P(("dp", "seq"), None),
    )
    return jax.shard_map(shards, mesh=mesh, in_specs=in_specs, out_specs=out_specs, check_vma=False)
```

```python
import itertools

import jax
import jax.numpy as jnp
from jax import lax
from jax.experimental import pallas as pl
from jax.experimental.pallas import tpu as pltpu
from jax.sharding import PartitionSpec as P

C = 1536
M = 384
TAPS = 5
STEP = 32
ROWS = 128
SEQ = 8
LENGTH = ROWS * SEQ
EDGE = TAPS // 2 * STEP
CAP = 16
JUNC = 448
PAIR = 2 * CAP
SLOTS = SEQ * PAIR
SIDE = 4
DP = SIDE * SIDE
OWNED = 12
BAND = 16
SHARE = DP * OWNED
YPART = 1024
PARTS = (slice(0, 128), slice(128, M))
WIDTHS = tuple(part.stop - part.start for part in PARTS)
UNITS = ((0, (0, 2), "z"), (0, (1, 3, 4), "y"), (1, (0, 2, 4), "z"), (1, (1, 3), "y"))
SIZES = tuple((len(taps), WIDTHS[part]) for part, taps, _ in UNITS)

TAP_ORDER = (0, 1, 4, 3, 2)
FAR = (4, 3, 5, 2, 6, 1, 7)

EPS = 1e-06
SLOPE = 0.7978845608028654
CUBIC = 0.044715

MESH = pl.DeviceIdType.MESH
bf16 = jnp.bfloat16
f32 = jnp.float32
i32 = jnp.int32


def dot(a, b):
    return jnp.dot(a, b, preferred_element_type=f32)


def dot_nt(a, b):
    return lax.dot_general(a, b, (((1,), (1,)), ((), ())), preferred_element_type=f32)


def dot_tn(a, b):
    return lax.dot_general(a, b, (((0,), (0,)), ((), ())), preferred_element_type=f32)


def one_hot(count, row):
    return lax.broadcasted_iota(i32, (count, row.shape[1]), 0) == row


def ones_of(mask):
    return jnp.where(mask, 1.0, 0.0).astype(bf16)


def gelu_parts(v):
    curved = jnp.tanh(SLOPE * (v + CUBIC * v * v * v))
    hidden = 0.5 * v * (1.0 + curved)
    slope = 0.5 * (1.0 + curved) + 0.5 * v * (1.0 - curved * curved) * SLOPE * (
        1.0 + 3.0 * CUBIC * v * v
    )
    return hidden, slope


def junction_matrices(s, don, acc, flags, grad):
    scaled = grad * flags.astype(f32) * C ** (-0.5)
    high = scaled.astype(bf16)
    low = (scaled - high.astype(f32)).astype(bf16)
    don_owner = don >> 7
    acc_owner = acc >> 7
    pairs = ones_of(one_hot(SEQ * SEQ, don_owner * SEQ + acc_owner))
    earlier = ones_of(
        lax.broadcasted_iota(i32, (JUNC, JUNC), 0) < lax.broadcasted_iota(i32, (JUNC, JUNC), 1)
    )
    counts = dot(pairs, earlier)
    rank = jnp.sum(pairs.astype(f32) * counts, axis=0, keepdims=True).astype(i32)
    don_here = don_owner == s
    acc_here = acc_owner == s
    don_at = one_hot(ROWS, don - s * ROWS)
    acc_at = one_hot(ROWS, acc - s * ROWS)
    send_don = ones_of(one_hot(SLOTS, jnp.where(don_here, acc_owner * PAIR + rank, -1)))
    send_acc = ones_of(one_hot(SLOTS, jnp.where(acc_here, don_owner * PAIR + CAP + rank, -1)))
    select = (dot_nt(send_don, ones_of(don_at)) + dot_nt(send_acc, ones_of(acc_at))).astype(bf16)
    came_don = ones_of(one_hot(SLOTS, jnp.where(acc_here, don_owner * PAIR + rank, -1)))
    came_acc = ones_of(one_hot(SLOTS, jnp.where(don_here, acc_owner * PAIR + CAP + rank, -1)))

    def placing(weight):
        wide = weight.astype(f32)
        at_acc = jnp.where(acc_at, wide, 0.0).astype(bf16)
        at_don = jnp.where(don_at, wide, 0.0).astype(bf16)
        return (dot_nt(at_acc, came_don) + dot_nt(at_don, came_acc)).astype(bf16)

    return select, jnp.concatenate([placing(high), placing(low)], axis=0)


def kernel(
    act_hbm,
    w_hbm,
    ow_hbm,
    cot_hbm,
    don_hbm,
    acc_hbm,
    flag_hbm,
    grad_hbm,
    block,
    result,
    cout,
    oout,
    act,
    w,
    ow,
    cot,
    don,
    acc,
    flag,
    grad,
    edge_send,
    edge_recv,
    xsend,
    xall,
    xedge,
    xhalo,
    window_y,
    window_z,
    gsend,
    grecv,
    hsend,
    hrecv,
    bsend,
    brecv,
    gall,
    gpad,
    cbuf,
    c1,
    c2,
    c3,
    osend_y,
    osend_x,
    osib_y,
    osib_x,
    obuf_y,
    obuf_x,
    o1_y,
    o1_x,
    o2_y,
    o2_x,
    o3_y,
    o3_x,
    oz,
    ozr,
    lsem,
    ssem,
    rsem,
):
    s = lax.axis_index("seq")
    d = lax.axis_index("dp")
    z, core = s // 2, s % 2
    y, x = d // SIDE, d % SIDE
    sibling = s + 1 - 2 * core
    ids = itertools.count()
    pending = []

    def push(src, dst, **device):
        i = next(ids)
        copy = pltpu.make_async_remote_copy(
            src_ref=src,
            dst_ref=dst,
            send_sem=ssem.at[i],
            recv_sem=rsem.at[i],
            device_id=device,
            device_id_type=MESH,
        )
        copy.start()
        pending.append(copy)
        return copy

    def seq_at(step):
        return lax.rem(s + step, SEQ)

    def x_at(step):
        return lax.rem(x + step, SIDE)

    def y_at(step):
        return lax.rem(y + step, SIDE)

    def x_peer(step):
        return y * SIDE + x_at(step)

    def y_peer(step):
        return y_at(step) * SIDE + x

    def z_at(step):
        return lax.rem(z + step, SIDE)

    loads = {}
    for i, (name, src, dst) in enumerate(
        (
            ("act", act_hbm.at[0], act),
            ("don", don_hbm, don),
            ("acc", acc_hbm, acc),
            ("flag", flag_hbm, flag),
            ("grad", grad_hbm, grad),
            *((f"w{tap}", w_hbm.at[tap], w.at[tap]) for tap in TAP_ORDER),
            ("ow", ow_hbm, ow),
            ("cot", cot_hbm.at[0], cot),
        )
    ):
        loads[name] = pltpu.make_async_copy(src, dst, lsem.at[i])
        loads[name].start()

    barrier = pltpu.get_barrier_semaphore()
    for step in range(1, SEQ):
        pl.semaphore_signal(barrier, inc=1, device_id={"seq": seq_at(step)}, device_id_type=MESH)
    for step in range(1, SIDE):
        pl.semaphore_signal(barrier, inc=1, device_id={"dp": y_peer(step)}, device_id_type=MESH)
        pl.semaphore_signal(barrier, inc=1, device_id={"dp": x_peer(step)}, device_id_type=MESH)
        pl.semaphore_signal(
            barrier, inc=1, device_id={"dp": x_peer(step), "seq": sibling}, device_id_type=MESH
        )

    loads["act"].wait()
    act_float = act[...].astype(f32)
    inverse = lax.rsqrt(jnp.mean(act_float * act_float, axis=-1, keepdims=True) + EPS)
    normed = (act_float * inverse).astype(bf16)

    me = x * 2 + core
    column = lax.broadcasted_iota(i32, (1, C), 1)
    owner, lane = column // SHARE, column % SHARE
    device = lane // OWNED
    channel = (
        (device // SIDE * SIDE + owner // 2) * (OWNED * SEQ)
        + (device % SIDE * 2 + owner % 2) * OWNED
        + lane % OWNED
    )
    grouped = dot(normed, ones_of(one_hot(C, channel)))
    left = lax.broadcasted_iota(i32, (STEP, 2 * SHARE), 1) < SHARE
    for upper_lower in range(2):
        for pair in range(SEQ // 2):
            both = grouped[
                2 * upper_lower * STEP : 2 * (upper_lower + 1) * STEP, pair * 2 * SHARE : (pair + 1) * 2 * SHARE
            ]
            upper, lower = both[:STEP], both[STEP:]
            xsend[upper_lower, 2 * pair] = jnp.where(left, upper, pltpu.roll(lower, SHARE, 1)).astype(bf16)
            xsend[upper_lower, 2 * pair + 1] = jnp.where(left, pltpu.roll(upper, SHARE, 1), lower).astype(
                bf16
            )
    xall[me] = xsend[:, me]
    pl.semaphore_wait(barrier, SEQ - 1 + 3 * (SIDE - 1))

    row_peers = [
        (step, turn) for step in (2, 1, 3) for turn in range(2)
    ]

    def row_device(step, turn):
        seq = sibling if turn else s
        return x_at(step) * 2 + lax.rem(core + turn, 2), dict(dp=x_peer(step), seq=seq)

    outer = lax.rem(s + SEQ - 1 + 2 * core, SEQ)
    edge_rows = push(xsend.at[core], xedge, seq=outer)

    x_copies = []
    for step, turn in row_peers:
        to, device_id = row_device(step, turn)
        x_copies.append(push(xsend.at[:, to], xall.at[me], **device_id))
    x_copies.append(push(xsend.at[:, x * 2 + 1 - core], xall.at[me], seq=sibling))
    taps = {}
    for tap in (0, 1):
        loads[f"w{tap}"].wait()
        taps[tap] = dot(normed, w[tap])
    half = ROWS // 2
    edge_send[0] = (
        taps[0][half:] + jnp.concatenate([taps[1][ROWS - STEP :], jnp.zeros((STEP, M), f32)], axis=0)
    ).astype(bf16)
    ahead = push(edge_send.at[0], edge_recv.at[0], seq=seq_at(1))
    for tap in (4, 3):
        loads[f"w{tap}"].wait()
        taps[tap] = dot(normed, w[tap])
    edge_send[1] = (
        taps[4][:half] + jnp.concatenate([jnp.zeros((STEP, M), f32), taps[3][:STEP]], axis=0)
    ).astype(bf16)
    behind = push(edge_send.at[1], edge_recv.at[1], seq=seq_at(SEQ - 1))
    for name in ("don", "acc", "flag", "grad"):
        loads[name].wait()
    select, place_both = junction_matrices(s, don[...], acc[...], flag[...], grad[...])

    def own_block(ref):
        return ref.at[pl.ds(pl.multiple_of(s * PAIR, PAIR), PAIR)]

    def send_slots(rows, out, into):
        out[...] = dot(select, rows).astype(bf16)
        own_block(into)[...] = own_block(out)[...]
        copies = []
        for step in FAR:
            peer = seq_at(step)
            src = out.at[pl.ds(pl.multiple_of(peer * PAIR, PAIR), PAIR)]
            copies.append(push(src, own_block(into), seq=peer))
        return copies

    def placed(ref):
        both = dot(place_both, ref[...])
        return both[:ROWS] + both[ROWS:]

    loads["ow"].wait()
    ow_value = ow[...]
    act_back = dot_nt(act[...], ow_value).astype(bf16)
    act_slots = send_slots(act_back, gsend, grecv)

    edge_rows.wait_recv()
    xhalo[me] = xedge[me]
    for step, turn in row_peers:
        to, device_id = row_device(step, turn)
        x_copies.append(push(xedge.at[to], xhalo.at[me], **device_id))
    x_copies.append(push(xedge.at[x * 2 + 1 - core], xhalo.at[me], seq=sibling))

    loads["w2"].wait()
    preact = dot(normed, w[2])
    preact = preact + jnp.concatenate(
        [
            taps[4][half:] + taps[3][STEP : STEP + half],
            jnp.concatenate([taps[3][STEP + half :], jnp.zeros((STEP, M), f32)], axis=0)
            + taps[0][:half]
            + taps[1][STEP : STEP + half],
        ],
        axis=0,
    )
    preact = preact + jnp.concatenate(
        [
            jnp.zeros((STEP, M), f32),
            taps[1][:STEP],
            jnp.zeros((half, M), f32),
        ],
        axis=0,
    )
    ahead.wait_recv()
    behind.wait_recv()
    preact = preact + jnp.concatenate(
        [
            jnp.where(s > 0, edge_recv[0].astype(f32), 0.0),
            jnp.where(s < SEQ - 1, edge_recv[1].astype(f32), 0.0),
        ],
        axis=0,
    )
    hidden_float, slope = gelu_parts(preact)
    hidden = hidden_float.astype(bf16)
    hidden_slots = send_slots(hidden, hsend, hrecv)

    block[0] = (act[...].astype(f32) + dot(hidden, ow_value)).astype(bf16)
    loads["cot"].wait()
    backs = dot_nt(jnp.concatenate([cot[...], ow_value], axis=0), ow_value)
    cot_back = backs[:ROWS]
    ow_square = backs[ROWS:].astype(bf16)

    for copy in act_slots:
        copy.wait_recv()
    cot_back = cot_back + placed(grecv)
    for copy in hidden_slots:
        copy.wait_recv()
    mixed = placed(hrecv).astype(bf16)
    grad_hidden = cot_back + dot(mixed, ow_square)
    grad_pre = (grad_hidden * slope).astype(bf16)
    own_rows = pl.ds(pl.multiple_of(me * ROWS, ROWS), ROWS)
    for part, columns in zip(gall, PARTS):
        part[own_rows] = grad_pre[:, columns]
    gpad[EDGE : EDGE + ROWS] = grad_pre

    def chunk(part, owner):
        return part.at[pl.ds(pl.multiple_of(owner * ROWS, ROWS), ROWS)]

    along, across = [], []

    def spread(part):
        along.append(
            [push(chunk(part, me), chunk(part, me), dp=x_peer(step)) for step in (2, 1, 3)]
        )
        across.append([push(chunk(part, me), chunk(part, me), seq=sibling)])

    def forward(i):
        for step, copy in ((1, along[i][1]), (3, along[i][2]), (2, along[i][0])):
            copy.wait_recv()
            owner = x_at(SIDE - step) * 2 + core
            across[i].append(push(chunk(gall[i], owner), chunk(gall[i], owner), seq=sibling))

    spread(gall[0])
    spread(gall[1])
    pad_copies = [
        push(gpad.at[ROWS : ROWS + EDGE], gpad.at[0:EDGE], seq=seq_at(1)),
        push(gpad.at[EDGE : 2 * EDGE], gpad.at[EDGE + ROWS :], seq=seq_at(SEQ - 1)),
    ]
    block_slots = send_slots(block[0], bsend, brecv)

    def ordered(first):
        lane = lax.broadcasted_iota(i32, (1, M), 1)
        half, rest = lane // (DP * OWNED), lane % (DP * OWNED)
        outer, rest = rest // (SIDE * OWNED), rest % (SIDE * OWNED)
        inner, rest = rest // OWNED, rest % OWNED
        device = outer * SIDE + inner if first == "y" else inner * SIDE + outer
        order = ones_of(one_hot(M, device * 3 * SEQ + rest // 3 * 6 + half * 3 + rest % 3))
        return dot(jnp.concatenate([hidden, mixed], axis=0), order).astype(bf16)

    def out_terms(first, columns):
        rows = jnp.concatenate([cot[:, columns], block[0, :, columns]], axis=0)
        terms = dot_tn(ordered(first), rows)
        return terms.astype(bf16).reshape(2, SIDE, SIDE * OWNED, columns.stop - columns.start)

    osend_y[...] = out_terms("y", slice(0, YPART))
    osend_x[...] = out_terms("x", slice(YPART, C))
    to_sibling = [
        push(osend_y.at[1 - core], osib_y, seq=sibling),
        push(osend_x.at[1 - core], osib_x, seq=sibling),
    ]

    for copy in to_sibling:
        copy.wait_recv()
    obuf_y[...] = (osend_y[core].astype(f32) + osib_y[...].astype(f32)).astype(bf16)
    obuf_x[...] = (osend_x[core].astype(f32) + osib_x[...].astype(f32)).astype(bf16)
    out_first = []
    for step in range(1, SIDE):
        out_first.append(push(obuf_y.at[y_at(step)], o1_y.at[step - 1], dp=y_at(step) * SIDE + x))
        out_first.append(push(obuf_x.at[x_at(step)], o1_x.at[step - 1], dp=y * SIDE + x_at(step)))

    def unpacked(came, first):
        lane = lax.broadcasted_iota(i32, (1, SHARE), 1)
        outer, rest = lane // (SIDE * OWNED), lane % (SIDE * OWNED)
        inner, row = rest // OWNED, rest % OWNED
        device = outer * SIDE + inner if first == "y" else inner * SIDE + outer
        flat = came.reshape(-1, 2 * SHARE)
        parts = [
            dot(flat, ones_of(one_hot(2 * SHARE, device * OWNED + row + SHARE * lower)))
            for lower in range(2)
        ]
        parts = [part.astype(bf16).reshape(-1, STEP, SHARE) for part in parts]
        return jnp.concatenate(parts, axis=1)

    def windows(first):
        middle = unpacked(xall[...], first).reshape(SIDE, 2 * ROWS, SHARE)
        sides = unpacked(xhalo[...], first).reshape(SIDE, 2, EDGE, SHARE)
        nothing = jnp.zeros((SIDE, EDGE, SHARE), bf16)
        return jnp.concatenate(
            [
                jnp.where(z > 0, sides[:, 0], nothing),
                middle,
                jnp.where(z < SIDE - 1, sides[:, 1], nothing),
            ],
            axis=1,
        )

    for copy in x_copies:
        copy.wait_recv()
    window_y[...] = windows("y")
    window_z[...] = windows("z")

    def zy_device(axis, step):
        if axis == "z":
            return z_at(step), dict(seq=seq_at(2 * step))
        return y_at(step), dict(dp=y_peer(step))

    def conv_terms(u):
        part, taps_here, first = UNITS[u]
        window = window_z if first == "z" else window_y
        for i, tap in enumerate(taps_here):
            rows = window[:, tap * STEP : tap * STEP + 2 * ROWS].reshape(LENGTH, SHARE)
            term = dot_tn(rows, gall[part][...])
            cbuf[u][i] = term.astype(bf16).reshape(SIDE, SIDE * OWNED, term.shape[1])
        copies = []
        for step in (2, 1, 3):
            at, peer = zy_device(first, step)
            copies.append(push(cbuf[u].at[:, at], c1[u].at[step - 1], **peer))
        return copies

    forward(0)
    for copy in across[0]:
        copy.wait_recv()
    conv_first = [conv_terms(0)]
    forward(1)
    conv_first.append(conv_terms(1))
    for copy in across[1]:
        copy.wait_recv()
    conv_first.append(conv_terms(2))
    conv_first.append(conv_terms(3))

    band = lax.broadcasted_iota(i32, (SIDE * BAND, SIDE * OWNED), 0)
    packed = lax.broadcasted_iota(i32, (SIDE * BAND, SIDE * OWNED), 1)
    spread_rows = ones_of((band // BAND * OWNED + band % BAND == packed) & (band % BAND < OWNED))

    def summed(own, came):
        total = own.astype(f32)
        for step in range(1, SIDE):
            total = total + came[step - 1].astype(f32)
        return total

    def banded(total):
        bands = dot(spread_rows, total.astype(bf16)).astype(bf16)
        return bands.reshape(SIDE, BAND, total.shape[1])

    for copy in out_first:
        copy.wait_recv()
    o2_y[...] = banded(summed(obuf_y[y], o1_y))
    o2_x[...] = banded(summed(obuf_x[x], o1_x))
    out_second = []
    for step in range(1, SIDE):
        out_second.append(push(o2_y.at[x_at(step)], o3_y.at[step - 1], dp=y * SIDE + x_at(step)))
        out_second.append(push(o2_x.at[y_at(step)], o3_x.at[step - 1], dp=y_at(step) * SIDE + x))

    for copy in pad_copies:
        copy.wait_recv()

    @pl.when(s == 0)
    def _():
        gpad[0:EDGE] = jnp.zeros((EDGE, M), bf16)

    @pl.when(s == SEQ - 1)
    def _():
        gpad[EDGE + ROWS :] = jnp.zeros((EDGE, M), bf16)

    grad_normed = jnp.zeros((ROWS, C), f32)
    for tap in range(TAPS):
        start = 2 * EDGE - tap * STEP
        grad_normed = grad_normed + dot_nt(gpad[start : start + ROWS], w[tap])

    conv_second = []
    for u, (part, taps_here, first) in enumerate(UNITS):
        for copy in conv_first[u]:
            copy.wait_recv()
        mine = z if first == "z" else y
        for i in range(len(taps_here)):
            total = cbuf[u][i, mine].astype(f32)
            for step in range(1, SIDE):
                total = total + c1[u][step - 1, i].astype(f32)
            c2[u][:, i] = banded(total)
        copies = []
        for step in (2, 1, 3):
            at, peer = zy_device("y" if first == "z" else "z", step)
            copies.append(push(c2[u].at[at], c3[u].at[step - 1], **peer))
        conv_second.append(copies)

    for copy in out_second:
        copy.wait_recv()
    total = jnp.concatenate([summed(o2_y[x], o3_y), summed(o2_x[y], o3_x)], axis=1)
    for level in range(SIDE):
        mine = total[3 * level : 3 * (level + 1)]
        quarters = [mine[:, i * M : (i + 1) * M] for i in range(SIDE)]
        oz[level] = jnp.concatenate([*quarters, jnp.zeros((BAND - OWNED, M), f32)], axis=0).astype(
            bf16
        )
    out_third = [
        push(oz.at[z_at(step)], ozr.at[step - 1], seq=seq_at(2 * step)) for step in range(1, SIDE)
    ]

    for copy in block_slots:
        copy.wait_recv()
    act_float = act[...].astype(f32)
    upstream = (cot[...].astype(f32) + placed(brecv)).astype(bf16)
    spread = jnp.mean(grad_normed * act_float, axis=-1, keepdims=True)
    result[0] = (
        upstream.astype(f32)
        + inverse * grad_normed
        - inverse * inverse * inverse * act_float * spread
    ).astype(bf16)
    for u, (part, taps_here, first) in enumerate(UNITS):
        for copy in conv_second[u]:
            copy.wait_recv()
        mine = y if first == "z" else z
        for i, tap in enumerate(taps_here):
            total = summed(c2[u][mine, i], c3[u].at[:, i])
            cout[tap, :, PARTS[part]] = total[:OWNED]

    for copy in out_third:
        copy.wait_recv()
    total = summed(oz[z], ozr)
    rows = jnp.concatenate([total[3 * i : 3 * (i + 1)] for i in range(SIDE)], axis=1)
    oout[...] = rows
    for copy in pending:
        copy.wait_send()


COPIES = 2 + 7 + 8 + 7 + 7 + 7 + 2 * (3 + 4) + 2 + 2 + 6 + 12 + 6 + 12 + 3


def store_kernel(*refs):
    came, left, sem = refs[:4], refs[4:8], refs[8]
    stores = [pltpu.make_async_copy(came[i], left[i], sem.at[i]) for i in range(4)]
    for store in stores:
        store.start()
    for store in stores:
        store.wait()


OUTPUTS = (
    jax.ShapeDtypeStruct((1, ROWS, C), bf16),
    jax.ShapeDtypeStruct((1, ROWS, C), bf16),
    jax.ShapeDtypeStruct((TAPS, OWNED, M), f32),
    jax.ShapeDtypeStruct((3, C), f32),
)


def shards(act, w, ow, cot, don, acc, flag, grad):
    any_space = pl.BlockSpec(memory_space=pl.ANY)
    vmem = pltpu.VMEM
    results = pl.pallas_call(
        kernel,
        name="block_step",
        out_shape=tuple(vmem(o.shape, o.dtype) for o in OUTPUTS),
        in_specs=[pl.BlockSpec(memory_space=pltpu.HBM)] * 8,
        out_specs=[pl.BlockSpec(memory_space=vmem)] * 4,
        scratch_shapes=[
            vmem((ROWS, C), bf16),
            vmem((TAPS, C, M), bf16),
            vmem((M, C), bf16),
            vmem((ROWS, C), bf16),
            vmem((1, JUNC), i32),
            vmem((1, JUNC), i32),
            vmem((1, JUNC), i32),
            vmem((1, JUNC), f32),
            vmem((2, EDGE, M), bf16),
            vmem((2, EDGE, M), bf16),
            vmem((2, SEQ, STEP, 2 * SHARE), bf16),
            vmem((SEQ, 2, STEP, 2 * SHARE), bf16),
            vmem((SEQ, STEP, 2 * SHARE), bf16),
            vmem((SEQ, STEP, 2 * SHARE), bf16),
            vmem((SIDE, 2 * (ROWS + EDGE), SHARE), bf16),
            vmem((SIDE, 2 * (ROWS + EDGE), SHARE), bf16),
            vmem((SLOTS, M), bf16),
            vmem((SLOTS, M), bf16),
            vmem((SLOTS, M), bf16),
            vmem((SLOTS, M), bf16),
            vmem((SLOTS, C), bf16),
            vmem((SLOTS, C), bf16),
            [vmem((LENGTH, width), bf16) for width in WIDTHS],
            vmem((ROWS + 2 * EDGE, M), bf16),
            [vmem((n, SIDE, SIDE * OWNED, width), bf16) for n, width in SIZES],
            [vmem((SIDE - 1, n, SIDE * OWNED, width), bf16) for n, width in SIZES],
            [vmem((SIDE, n, BAND, width), bf16) for n, width in SIZES],
            [vmem((SIDE - 1, n, BAND, width), bf16) for n, width in SIZES],
            vmem((2, SIDE, SIDE * OWNED, YPART), bf16),
            vmem((2, SIDE, SIDE * OWNED, C - YPART), bf16),
            vmem((SIDE, SIDE * OWNED, YPART), bf16),
            vmem((SIDE, SIDE * OWNED, C - YPART), bf16),
            vmem((SIDE, SIDE * OWNED, YPART), bf16),
            vmem((SIDE, SIDE * OWNED, C - YPART), bf16),
            vmem((SIDE - 1, SIDE * OWNED, YPART), bf16),
            vmem((SIDE - 1, SIDE * OWNED, C - YPART), bf16),
            vmem((SIDE, BAND, YPART), bf16),
            vmem((SIDE, BAND, C - YPART), bf16),
            vmem((SIDE - 1, BAND, YPART), bf16),
            vmem((SIDE - 1, BAND, C - YPART), bf16),
            vmem((SIDE, BAND, M), bf16),
            vmem((SIDE - 1, BAND, M), bf16),
            pltpu.SemaphoreType.DMA((12,)),
            pltpu.SemaphoreType.DMA((COPIES,)),
            pltpu.SemaphoreType.DMA((COPIES,)),
        ],
        compiler_params=pltpu.CompilerParams(
            collective_id=0, has_side_effects=True, vmem_limit_bytes=56 * 1024 * 1024
        ),
    )(act, w, ow, cot, don, acc, flag, grad)
    return pl.pallas_call(
        store_kernel,
        name="store_results",
        out_shape=OUTPUTS,
        in_specs=[pl.BlockSpec(memory_space=vmem)] * 4,
        out_specs=[any_space] * 4,
        scratch_shapes=[pltpu.SemaphoreType.DMA((4,))],
    )(*(pltpu.with_memory_space_constraint(r, pltpu.VMEM) for r in results))


def solution(mesh):
    in_specs = (
        P("dp", "seq", None),
        P(),
        P(),
        P("dp", "seq", None),
        P("dp", None),
        P("dp", None),
        P("dp", None),
        P("dp", None),
    )
    out_specs = (
        P("dp", "seq", None),
        P("dp", "seq", None),
        P(None, ("dp", "seq"), None),
        P(("dp", "seq"), None),
    )
    return jax.shard_map(shards, mesh=mesh, in_specs=in_specs, out_specs=out_specs, check_vma=False)
```

```python
import itertools

import jax
import jax.numpy as jnp
from jax import lax
from jax.experimental import pallas as pl
from jax.experimental.pallas import tpu as pltpu
from jax.sharding import PartitionSpec as P

C = 1536
M = 384
TAPS = 5
STEP = 32
ROWS = 128
SEQ = 8
LENGTH = ROWS * SEQ
EDGE = TAPS // 2 * STEP
CAP = 16
JUNC = 448
PAIR = 2 * CAP
SLOTS = SEQ * PAIR
SIDE = 4
DP = SIDE * SIDE
OWNED = 12
BAND = 16
SHARE = DP * OWNED
YPART = 1024
PARTS = (slice(0, 128), slice(128, M))
WIDTHS = tuple(part.stop - part.start for part in PARTS)
UNITS = ((0, (0, 2), "z"), (0, (1, 3, 4), "y"), (1, (0, 2, 4), "z"), (1, (1, 3), "y"))
SIZES = tuple((len(taps), WIDTHS[part]) for part, taps, _ in UNITS)

TAP_ORDER = (0, 1, 4, 3, 2)
FAR = (4, 3, 5, 2, 6, 1, 7)

EPS = 1e-06
SLOPE = 0.7978845608028654
CUBIC = 0.044715

MESH = pl.DeviceIdType.MESH
bf16 = jnp.bfloat16
f32 = jnp.float32
i32 = jnp.int32


def dot(a, b):
    return jnp.dot(a, b, preferred_element_type=f32)


def dot_nt(a, b):
    return lax.dot_general(a, b, (((1,), (1,)), ((), ())), preferred_element_type=f32)


def dot_tn(a, b):
    return lax.dot_general(a, b, (((0,), (0,)), ((), ())), preferred_element_type=f32)


def one_hot(count, row):
    return lax.broadcasted_iota(i32, (count, row.shape[1]), 0) == row


def ones_of(mask):
    return jnp.where(mask, 1.0, 0.0).astype(bf16)


def gelu_parts(v):
    curved = jnp.tanh(SLOPE * (v + CUBIC * v * v * v))
    hidden = 0.5 * v * (1.0 + curved)
    slope = 0.5 * (1.0 + curved) + 0.5 * v * (1.0 - curved * curved) * SLOPE * (
        1.0 + 3.0 * CUBIC * v * v
    )
    return hidden, slope


def junction_matrices(s, don, acc, flags, grad):
    scaled = grad * flags.astype(f32) * C ** (-0.5)
    high = scaled.astype(bf16)
    low = (scaled - high.astype(f32)).astype(bf16)
    don_owner = don >> 7
    acc_owner = acc >> 7
    pairs = ones_of(one_hot(SEQ * SEQ, don_owner * SEQ + acc_owner))
    earlier = ones_of(
        lax.broadcasted_iota(i32, (JUNC, JUNC), 0) < lax.broadcasted_iota(i32, (JUNC, JUNC), 1)
    )
    counts = dot(pairs, earlier)
    rank = jnp.sum(pairs.astype(f32) * counts, axis=0, keepdims=True).astype(i32)
    don_here = don_owner == s
    acc_here = acc_owner == s
    don_at = one_hot(ROWS, don - s * ROWS)
    acc_at = one_hot(ROWS, acc - s * ROWS)
    send_don = ones_of(one_hot(SLOTS, jnp.where(don_here, acc_owner * PAIR + rank, -1)))
    send_acc = ones_of(one_hot(SLOTS, jnp.where(acc_here, don_owner * PAIR + CAP + rank, -1)))
    select = (dot_nt(send_don, ones_of(don_at)) + dot_nt(send_acc, ones_of(acc_at))).astype(bf16)
    came_don = ones_of(one_hot(SLOTS, jnp.where(acc_here, don_owner * PAIR + rank, -1)))
    came_acc = ones_of(one_hot(SLOTS, jnp.where(don_here, acc_owner * PAIR + CAP + rank, -1)))

    def placing(weight):
        wide = weight.astype(f32)
        at_acc = jnp.where(acc_at, wide, 0.0).astype(bf16)
        at_don = jnp.where(don_at, wide, 0.0).astype(bf16)
        return (dot_nt(at_acc, came_don) + dot_nt(at_don, came_acc)).astype(bf16)

    return select, jnp.concatenate([placing(high), placing(low)], axis=0)


def kernel(
    act_hbm,
    w_hbm,
    ow_hbm,
    cot_hbm,
    don_hbm,
    acc_hbm,
    flag_hbm,
    grad_hbm,
    block,
    result,
    cout,
    oout,
    act,
    w,
    ow,
    cot,
    don,
    acc,
    flag,
    grad,
    edge_send,
    edge_recv,
    xsend,
    xall,
    xedge,
    xhalo,
    window_y,
    window_z,
    gsend,
    grecv,
    hsend,
    hrecv,
    bsend,
    brecv,
    gall,
    gpad,
    cbuf,
    c1,
    c2,
    c3,
    osend_y,
    osend_x,
    osib_y,
    osib_x,
    obuf_y,
    obuf_x,
    o1_y,
    o1_x,
    o2_y,
    o2_x,
    o3_y,
    o3_x,
    oz,
    ozr,
    lsem,
    ssem,
    rsem,
):
    s = lax.axis_index("seq")
    d = lax.axis_index("dp")
    z, core = s // 2, s % 2
    y, x = d // SIDE, d % SIDE
    sibling = s + 1 - 2 * core
    ids = itertools.count()
    pending = []

    def push(src, dst, **device):
        i = next(ids)
        copy = pltpu.make_async_remote_copy(
            src_ref=src,
            dst_ref=dst,
            send_sem=ssem.at[i],
            recv_sem=rsem.at[i],
            device_id=device,
            device_id_type=MESH,
        )
        copy.start()
        pending.append(copy)
        return copy

    def seq_at(step):
        return lax.rem(s + step, SEQ)

    def x_at(step):
        return lax.rem(x + step, SIDE)

    def y_at(step):
        return lax.rem(y + step, SIDE)

    def x_peer(step):
        return y * SIDE + x_at(step)

    def y_peer(step):
        return y_at(step) * SIDE + x

    def z_at(step):
        return lax.rem(z + step, SIDE)

    loads = {}
    for i, (name, src, dst) in enumerate(
        (
            ("act", act_hbm.at[0], act),
            ("don", don_hbm, don),
            ("acc", acc_hbm, acc),
            ("flag", flag_hbm, flag),
            ("grad", grad_hbm, grad),
            *((f"w{tap}", w_hbm.at[tap], w.at[tap]) for tap in TAP_ORDER),
            ("ow", ow_hbm, ow),
            ("cot", cot_hbm.at[0], cot),
        )
    ):
        loads[name] = pltpu.make_async_copy(src, dst, lsem.at[i])
        if name == "act":
            loads[name].start()

    barrier = pltpu.get_barrier_semaphore()
    for step in range(1, SEQ):
        pl.semaphore_signal(barrier, inc=1, device_id={"seq": seq_at(step)}, device_id_type=MESH)
    for step in range(1, SIDE):
        pl.semaphore_signal(barrier, inc=1, device_id={"dp": y_peer(step)}, device_id_type=MESH)
        pl.semaphore_signal(barrier, inc=1, device_id={"dp": x_peer(step)}, device_id_type=MESH)
        pl.semaphore_signal(
            barrier, inc=1, device_id={"dp": x_peer(step), "seq": sibling}, device_id_type=MESH
        )

    for name in list(loads)[1:]:
        loads[name].start()

    loads["act"].wait()
    act_float = act[...].astype(f32)
    inverse = lax.rsqrt(jnp.mean(act_float * act_float, axis=-1, keepdims=True) + EPS)
    normed = (act_float * inverse).astype(bf16)

    me = x * 2 + core
    column = lax.broadcasted_iota(i32, (1, C), 1)
    owner, lane = column // SHARE, column % SHARE
    device = lane // OWNED
    channel = (
        (device // SIDE * SIDE + owner // 2) * (OWNED * SEQ)
        + (device % SIDE * 2 + owner % 2) * OWNED
        + lane % OWNED
    )
    grouped = dot(normed, ones_of(one_hot(C, channel)))
    left = lax.broadcasted_iota(i32, (STEP, 2 * SHARE), 1) < SHARE
    for upper_lower in range(2):
        for pair in range(SEQ // 2):
            both = grouped[
                2 * upper_lower * STEP : 2 * (upper_lower + 1) * STEP, pair * 2 * SHARE : (pair + 1) * 2 * SHARE
            ]
            upper, lower = both[:STEP], both[STEP:]
            xsend[upper_lower, 2 * pair] = jnp.where(left, upper, pltpu.roll(lower, SHARE, 1)).astype(bf16)
            xsend[upper_lower, 2 * pair + 1] = jnp.where(left, pltpu.roll(upper, SHARE, 1), lower).astype(
                bf16
            )
    xall[me] = xsend[:, me]
    pl.semaphore_wait(barrier, SEQ - 1 + 3 * (SIDE - 1))

    row_peers = [
        (step, turn) for step in (2, 1, 3) for turn in range(2)
    ]

    def row_device(step, turn):
        seq = sibling if turn else s
        return x_at(step) * 2 + lax.rem(core + turn, 2), dict(dp=x_peer(step), seq=seq)

    outer = lax.rem(s + SEQ - 1 + 2 * core, SEQ)
    edge_rows = push(xsend.at[core], xedge, seq=outer)

    x_copies = []
    for step, turn in row_peers:
        to, device_id = row_device(step, turn)
        x_copies.append(push(xsend.at[:, to], xall.at[me], **device_id))
    x_copies.append(push(xsend.at[:, x * 2 + 1 - core], xall.at[me], seq=sibling))
    taps = {}
    for tap in (0, 1):
        loads[f"w{tap}"].wait()
        taps[tap] = dot(normed, w[tap])
    half = ROWS // 2
    edge_send[0] = (
        taps[0][half:] + jnp.concatenate([taps[1][ROWS - STEP :], jnp.zeros((STEP, M), f32)], axis=0)
    ).astype(bf16)
    ahead = push(edge_send.at[0], edge_recv.at[0], seq=seq_at(1))
    for tap in (4, 3):
        loads[f"w{tap}"].wait()
        taps[tap] = dot(normed, w[tap])
    edge_send[1] = (
        taps[4][:half] + jnp.concatenate([jnp.zeros((STEP, M), f32), taps[3][:STEP]], axis=0)
    ).astype(bf16)
    behind = push(edge_send.at[1], edge_recv.at[1], seq=seq_at(SEQ - 1))
    for name in ("don", "acc", "flag", "grad"):
        loads[name].wait()
    select, place_both = junction_matrices(s, don[...], acc[...], flag[...], grad[...])

    def own_block(ref):
        return ref.at[pl.ds(pl.multiple_of(s * PAIR, PAIR), PAIR)]

    def send_slots(rows, out, into):
        out[...] = dot(select, rows).astype(bf16)
        own_block(into)[...] = own_block(out)[...]
        copies = []
        for step in FAR:
            peer = seq_at(step)
            src = out.at[pl.ds(pl.multiple_of(peer * PAIR, PAIR), PAIR)]
            copies.append(push(src, own_block(into), seq=peer))
        return copies

    def placed(ref):
        both = dot(place_both, ref[...])
        return both[:ROWS] + both[ROWS:]

    loads["ow"].wait()
    ow_value = ow[...]
    act_back = dot_nt(act[...], ow_value).astype(bf16)
    act_slots = send_slots(act_back, gsend, grecv)

    edge_rows.wait_recv()
    xhalo[me] = xedge[me]
    for step, turn in row_peers:
        to, device_id = row_device(step, turn)
        x_copies.append(push(xedge.at[to], xhalo.at[me], **device_id))
    x_copies.append(push(xedge.at[x * 2 + 1 - core], xhalo.at[me], seq=sibling))

    loads["w2"].wait()
    preact = dot(normed, w[2])
    preact = preact + jnp.concatenate(
        [
            taps[4][half:] + taps[3][STEP : STEP + half],
            jnp.concatenate([taps[3][STEP + half :], jnp.zeros((STEP, M), f32)], axis=0)
            + taps[0][:half]
            + taps[1][STEP : STEP + half],
        ],
        axis=0,
    )
    preact = preact + jnp.concatenate(
        [
            jnp.zeros((STEP, M), f32),
            taps[1][:STEP],
            jnp.zeros((half, M), f32),
        ],
        axis=0,
    )
    ahead.wait_recv()
    behind.wait_recv()
    preact = preact + jnp.concatenate(
        [
            jnp.where(s > 0, edge_recv[0].astype(f32), 0.0),
            jnp.where(s < SEQ - 1, edge_recv[1].astype(f32), 0.0),
        ],
        axis=0,
    )
    hidden_float, slope = gelu_parts(preact)
    hidden = hidden_float.astype(bf16)
    hidden_slots = send_slots(hidden, hsend, hrecv)

    block[0] = (act[...].astype(f32) + dot(hidden, ow_value)).astype(bf16)
    loads["cot"].wait()
    backs = dot_nt(jnp.concatenate([cot[...], ow_value], axis=0), ow_value)
    cot_back = backs[:ROWS]
    ow_square = backs[ROWS:].astype(bf16)

    for copy in act_slots:
        copy.wait_recv()
    cot_back = cot_back + placed(grecv)
    for copy in hidden_slots:
        copy.wait_recv()
    mixed = placed(hrecv).astype(bf16)
    grad_hidden = cot_back + dot(mixed, ow_square)
    grad_pre = (grad_hidden * slope).astype(bf16)
    own_rows = pl.ds(pl.multiple_of(me * ROWS, ROWS), ROWS)
    for part, columns in zip(gall, PARTS):
        part[own_rows] = grad_pre[:, columns]
    gpad[EDGE : EDGE + ROWS] = grad_pre

    def chunk(part, owner):
        return part.at[pl.ds(pl.multiple_of(owner * ROWS, ROWS), ROWS)]

    along, across = [], []

    def spread(part):
        along.append(
            [push(chunk(part, me), chunk(part, me), dp=x_peer(step)) for step in (2, 1, 3)]
        )
        across.append([push(chunk(part, me), chunk(part, me), seq=sibling)])

    def forward(i):
        for step, copy in ((1, along[i][1]), (3, along[i][2]), (2, along[i][0])):
            copy.wait_recv()
            owner = x_at(SIDE - step) * 2 + core
            across[i].append(push(chunk(gall[i], owner), chunk(gall[i], owner), seq=sibling))

    spread(gall[0])
    spread(gall[1])
    pad_copies = [
        push(gpad.at[ROWS : ROWS + EDGE], gpad.at[0:EDGE], seq=seq_at(1)),
        push(gpad.at[EDGE : 2 * EDGE], gpad.at[EDGE + ROWS :], seq=seq_at(SEQ - 1)),
    ]
    block_slots = send_slots(block[0], bsend, brecv)

    def ordered(first):
        lane = lax.broadcasted_iota(i32, (1, M), 1)
        half, rest = lane // (DP * OWNED), lane % (DP * OWNED)
        outer, rest = rest // (SIDE * OWNED), rest % (SIDE * OWNED)
        inner, rest = rest // OWNED, rest % OWNED
        device = outer * SIDE + inner if first == "y" else inner * SIDE + outer
        order = ones_of(one_hot(M, device * 3 * SEQ + rest // 3 * 6 + half * 3 + rest % 3))
        return dot(jnp.concatenate([hidden, mixed], axis=0), order).astype(bf16)

    def out_terms(first, columns):
        rows = jnp.concatenate([cot[:, columns], block[0, :, columns]], axis=0)
        terms = dot_tn(ordered(first), rows)
        return terms.astype(bf16).reshape(2, SIDE, SIDE * OWNED, columns.stop - columns.start)

    osend_y[...] = out_terms("y", slice(0, YPART))
    osend_x[...] = out_terms("x", slice(YPART, C))
    to_sibling = [
        push(osend_y.at[1 - core], osib_y, seq=sibling),
        push(osend_x.at[1 - core], osib_x, seq=sibling),
    ]

    for copy in to_sibling:
        copy.wait_recv()
    obuf_y[...] = (osend_y[core].astype(f32) + osib_y[...].astype(f32)).astype(bf16)
    obuf_x[...] = (osend_x[core].astype(f32) + osib_x[...].astype(f32)).astype(bf16)
    out_first = []
    for step in range(1, SIDE):
        out_first.append(push(obuf_y.at[y_at(step)], o1_y.at[step - 1], dp=y_at(step) * SIDE + x))
        out_first.append(push(obuf_x.at[x_at(step)], o1_x.at[step - 1], dp=y * SIDE + x_at(step)))

    def unpacked(came, first):
        lane = lax.broadcasted_iota(i32, (1, SHARE), 1)
        outer, rest = lane // (SIDE * OWNED), lane % (SIDE * OWNED)
        inner, row = rest // OWNED, rest % OWNED
        device = outer * SIDE + inner if first == "y" else inner * SIDE + outer
        flat = came.reshape(-1, 2 * SHARE)
        parts = [
            dot(flat, ones_of(one_hot(2 * SHARE, device * OWNED + row + SHARE * lower)))
            for lower in range(2)
        ]
        parts = [part.astype(bf16).reshape(-1, STEP, SHARE) for part in parts]
        return jnp.concatenate(parts, axis=1)

    def windows(first):
        middle = unpacked(xall[...], first).reshape(SIDE, 2 * ROWS, SHARE)
        sides = unpacked(xhalo[...], first).reshape(SIDE, 2, EDGE, SHARE)
        nothing = jnp.zeros((SIDE, EDGE, SHARE), bf16)
        return jnp.concatenate(
            [
                jnp.where(z > 0, sides[:, 0], nothing),
                middle,
                jnp.where(z < SIDE - 1, sides[:, 1], nothing),
            ],
            axis=1,
        )

    for copy in x_copies:
        copy.wait_recv()
    window_y[...] = windows("y")
    window_z[...] = windows("z")

    def zy_device(axis, step):
        if axis == "z":
            return z_at(step), dict(seq=seq_at(2 * step))
        return y_at(step), dict(dp=y_peer(step))

    def conv_terms(u):
        part, taps_here, first = UNITS[u]
        window = window_z if first == "z" else window_y
        for i, tap in enumerate(taps_here):
            rows = window[:, tap * STEP : tap * STEP + 2 * ROWS].reshape(LENGTH, SHARE)
            term = dot_tn(rows, gall[part][...])
            cbuf[u][i] = term.astype(bf16).reshape(SIDE, SIDE * OWNED, term.shape[1])
        copies = []
        for step in (2, 1, 3):
            at, peer = zy_device(first, step)
            copies.append(push(cbuf[u].at[:, at], c1[u].at[step - 1], **peer))
        return copies

    forward(0)
    for copy in across[0]:
        copy.wait_recv()
    conv_first = [conv_terms(0)]
    forward(1)
    conv_first.append(conv_terms(1))
    for copy in across[1]:
        copy.wait_recv()
    conv_first.append(conv_terms(2))
    conv_first.append(conv_terms(3))

    band = lax.broadcasted_iota(i32, (SIDE * BAND, SIDE * OWNED), 0)
    packed = lax.broadcasted_iota(i32, (SIDE * BAND, SIDE * OWNED), 1)
    spread_rows = ones_of((band // BAND * OWNED + band % BAND == packed) & (band % BAND < OWNED))

    def summed(own, came):
        total = own.astype(f32)
        for step in range(1, SIDE):
            total = total + came[step - 1].astype(f32)
        return total

    def banded(total):
        bands = dot(spread_rows, total.astype(bf16)).astype(bf16)
        return bands.reshape(SIDE, BAND, total.shape[1])

    for copy in out_first:
        copy.wait_recv()
    o2_y[...] = banded(summed(obuf_y[y], o1_y))
    o2_x[...] = banded(summed(obuf_x[x], o1_x))
    out_second = []
    for step in range(1, SIDE):
        out_second.append(push(o2_y.at[x_at(step)], o3_y.at[step - 1], dp=y * SIDE + x_at(step)))
        out_second.append(push(o2_x.at[y_at(step)], o3_x.at[step - 1], dp=y_at(step) * SIDE + x))

    for copy in pad_copies:
        copy.wait_recv()

    @pl.when(s == 0)
    def _():
        gpad[0:EDGE] = jnp.zeros((EDGE, M), bf16)

    @pl.when(s == SEQ - 1)
    def _():
        gpad[EDGE + ROWS :] = jnp.zeros((EDGE, M), bf16)

    grad_normed = jnp.zeros((ROWS, C), f32)
    for tap in range(TAPS):
        start = 2 * EDGE - tap * STEP
        grad_normed = grad_normed + dot_nt(gpad[start : start + ROWS], w[tap])

    conv_second = []
    for u, (part, taps_here, first) in enumerate(UNITS):
        for copy in conv_first[u]:
            copy.wait_recv()
        mine = z if first == "z" else y
        for i in range(len(taps_here)):
            total = cbuf[u][i, mine].astype(f32)
            for step in range(1, SIDE):
                total = total + c1[u][step - 1, i].astype(f32)
            c2[u][:, i] = banded(total)
        copies = []
        for step in (2, 1, 3):
            at, peer = zy_device("y" if first == "z" else "z", step)
            copies.append(push(c2[u].at[at], c3[u].at[step - 1], **peer))
        conv_second.append(copies)

    for copy in out_second:
        copy.wait_recv()
    total = jnp.concatenate([summed(o2_y[x], o3_y), summed(o2_x[y], o3_x)], axis=1)
    for level in range(SIDE):
        mine = total[3 * level : 3 * (level + 1)]
        quarters = [mine[:, i * M : (i + 1) * M] for i in range(SIDE)]
        oz[level] = jnp.concatenate([*quarters, jnp.zeros((BAND - OWNED, M), f32)], axis=0).astype(
            bf16
        )
    out_third = [
        push(oz.at[z_at(step)], ozr.at[step - 1], seq=seq_at(2 * step)) for step in range(1, SIDE)
    ]

    for copy in block_slots:
        copy.wait_recv()
    act_float = act[...].astype(f32)
    upstream = (cot[...].astype(f32) + placed(brecv)).astype(bf16)
    spread = jnp.mean(grad_normed * act_float, axis=-1, keepdims=True)
    result[0] = (
        upstream.astype(f32)
        + inverse * grad_normed
        - inverse * inverse * inverse * act_float * spread
    ).astype(bf16)
    for u, (part, taps_here, first) in enumerate(UNITS):
        for copy in conv_second[u]:
            copy.wait_recv()
        mine = y if first == "z" else z
        for i, tap in enumerate(taps_here):
            total = summed(c2[u][mine, i], c3[u].at[:, i])
            cout[tap, :, PARTS[part]] = total[:OWNED]

    for copy in out_third:
        copy.wait_recv()
    total = summed(oz[z], ozr)
    rows = jnp.concatenate([total[3 * i : 3 * (i + 1)] for i in range(SIDE)], axis=1)
    oout[...] = rows
    for copy in pending:
        copy.wait_send()


COPIES = 2 + 7 + 8 + 7 + 7 + 7 + 2 * (3 + 4) + 2 + 2 + 6 + 12 + 6 + 12 + 3


def store_kernel(*refs):
    came, left, sem = refs[:4], refs[4:8], refs[8]
    pieces = [
        (came[i].at[:, rows], left[i].at[:, rows])
        for rows in (pl.ds(start, STEP) for start in range(0, ROWS, STEP))
        for i in range(2)
    ] + [(came[i], left[i]) for i in range(2, 4)]
    stores = [pltpu.make_async_copy(*piece, sem.at[i]) for i, piece in enumerate(pieces)]
    for store in stores:
        store.start()
    for store in stores:
        store.wait()


OUTPUTS = (
    jax.ShapeDtypeStruct((1, ROWS, C), bf16),
    jax.ShapeDtypeStruct((1, ROWS, C), bf16),
    jax.ShapeDtypeStruct((TAPS, OWNED, M), f32),
    jax.ShapeDtypeStruct((3, C), f32),
)


def shards(act, w, ow, cot, don, acc, flag, grad):
    any_space = pl.BlockSpec(memory_space=pl.ANY)
    vmem = pltpu.VMEM
    results = pl.pallas_call(
        kernel,
        name="block_step",
        out_shape=tuple(vmem(o.shape, o.dtype) for o in OUTPUTS),
        in_specs=[pl.BlockSpec(memory_space=pltpu.HBM)] * 8,
        out_specs=[pl.BlockSpec(memory_space=vmem)] * 4,
        scratch_shapes=[
            vmem((ROWS, C), bf16),
            vmem((TAPS, C, M), bf16),
            vmem((M, C), bf16),
            vmem((ROWS, C), bf16),
            vmem((1, JUNC), i32),
            vmem((1, JUNC), i32),
            vmem((1, JUNC), i32),
            vmem((1, JUNC), f32),
            vmem((2, EDGE, M), bf16),
            vmem((2, EDGE, M), bf16),
            vmem((2, SEQ, STEP, 2 * SHARE), bf16),
            vmem((SEQ, 2, STEP, 2 * SHARE), bf16),
            vmem((SEQ, STEP, 2 * SHARE), bf16),
            vmem((SEQ, STEP, 2 * SHARE), bf16),
            vmem((SIDE, 2 * (ROWS + EDGE), SHARE), bf16),
            vmem((SIDE, 2 * (ROWS + EDGE), SHARE), bf16),
            vmem((SLOTS, M), bf16),
            vmem((SLOTS, M), bf16),
            vmem((SLOTS, M), bf16),
            vmem((SLOTS, M), bf16),
            vmem((SLOTS, C), bf16),
            vmem((SLOTS, C), bf16),
            [vmem((LENGTH, width), bf16) for width in WIDTHS],
            vmem((ROWS + 2 * EDGE, M), bf16),
            [vmem((n, SIDE, SIDE * OWNED, width), bf16) for n, width in SIZES],
            [vmem((SIDE - 1, n, SIDE * OWNED, width), bf16) for n, width in SIZES],
            [vmem((SIDE, n, BAND, width), bf16) for n, width in SIZES],
            [vmem((SIDE - 1, n, BAND, width), bf16) for n, width in SIZES],
            vmem((2, SIDE, SIDE * OWNED, YPART), bf16),
            vmem((2, SIDE, SIDE * OWNED, C - YPART), bf16),
            vmem((SIDE, SIDE * OWNED, YPART), bf16),
            vmem((SIDE, SIDE * OWNED, C - YPART), bf16),
            vmem((SIDE, SIDE * OWNED, YPART), bf16),
            vmem((SIDE, SIDE * OWNED, C - YPART), bf16),
            vmem((SIDE - 1, SIDE * OWNED, YPART), bf16),
            vmem((SIDE - 1, SIDE * OWNED, C - YPART), bf16),
            vmem((SIDE, BAND, YPART), bf16),
            vmem((SIDE, BAND, C - YPART), bf16),
            vmem((SIDE - 1, BAND, YPART), bf16),
            vmem((SIDE - 1, BAND, C - YPART), bf16),
            vmem((SIDE, BAND, M), bf16),
            vmem((SIDE - 1, BAND, M), bf16),
            pltpu.SemaphoreType.DMA((12,)),
            pltpu.SemaphoreType.DMA((COPIES,)),
            pltpu.SemaphoreType.DMA((COPIES,)),
        ],
        compiler_params=pltpu.CompilerParams(
            collective_id=0, has_side_effects=True, vmem_limit_bytes=56 * 1024 * 1024
        ),
    )(act, w, ow, cot, don, acc, flag, grad)
    return pl.pallas_call(
        store_kernel,
        name="store_results",
        out_shape=OUTPUTS,
        in_specs=[pl.BlockSpec(memory_space=vmem)] * 4,
        out_specs=[any_space] * 4,
        scratch_shapes=[pltpu.SemaphoreType.DMA((2 * (ROWS // STEP) + 2,))],
    )(*(pltpu.with_memory_space_constraint(r, pltpu.VMEM) for r in results))


def solution(mesh):
    in_specs = (
        P("dp", "seq", None),
        P(),
        P(),
        P("dp", "seq", None),
        P("dp", None),
        P("dp", None),
        P("dp", None),
        P("dp", None),
    )
    out_specs = (
        P("dp", "seq", None),
        P("dp", "seq", None),
        P(None, ("dp", "seq"), None),
        P(("dp", "seq"), None),
    )
    return jax.shard_map(shards, mesh=mesh, in_specs=in_specs, out_specs=out_specs, check_vma=False)
```
